256 devices in a mesh: leaf: 256 (over y, x, z, core).
Axes of the slice: x: 4, y: 4, z: 8, core: 2. Of those that a mesh axis runs over, the one named last changes fastest.
Arguments:
- coords: float32 [16, 1048576], P(None, 'leaf'), may hold values from -128 to 128
- solution: float32 [16, 1048576], P(None, 'leaf'), may hold values from -6 to 6
- residual: float32 [16, 1048576], P(None, 'leaf'), may hold values from -128 to 128
- direction: float32 [16, 1048576], P(None, 'leaf'), may hold values from -128 to 128
- order: int32 [1048576], P('leaf'), may hold values from 0 to 4095, as said below
- leaf_skel: int32 [512, 256], P('leaf'), may hold values from 0 to 2047, as said below
- local_skel: int32 [256, 256], P('leaf'), may hold values from 0 to 511, as said below
- upper_skel: int32 [7, 256, 256], P(None, 'leaf'), may hold values from 0 to 511, as said below
Outputs:
- new_solution: float32 [16, 1048576], P(None, 'leaf')
- new_residual: float32 [16, 1048576], P(None, 'leaf')
- new_direction: float32 [16, 1048576], P(None, 'leaf')
The draws below stay inside these ranges and needn't reach their ends.
Inputs may be any that keep to these rules, and one draw needn't show every extreme that they name: `order`: each device's block of 4096 entries is a permutation of 0 to 4095. `leaf_skel`: the 256 entries of a row are distinct. `local_skel`: the 256 entries of a row are distinct. `upper_skel`: the 256 entries of a row are distinct; for each u, the rows of devices whose indices agree after dropping the lowest u + 1 bits are equal.
All inputs are finite; a program needn't handle non-finite values.
Results may differ from the reference program's by a relative error of at most 0.0003.
Values sent between devices are 32-bit elements; how exact they have to be, the bound alone decides.
A program may use at most 320 MiB of HBM per device.

```python
import math
import jax
import jax.numpy as jnp
from jax import lax

DIM = 16
LEAF = 2048
RANK = 256
NRHS = 16
LEAVES_DEV = 2
ITERS = 4
ULEV = 7
PTS_DEV = 4096
NLEAVES = 512
POINTS = 1048576
N_LEAF = 256


def block_orders(key):
    keys = jax.random.split(jax.random.fold_in(key, 101), N_LEAF)
    return jax.vmap(lambda sub_key: jax.random.permutation(sub_key, PTS_DEV))(keys).astype(jnp.int32)


def input_slots(key):
    device_ids = jnp.arange(POINTS, dtype=jnp.int32) // PTS_DEV
    return device_ids * PTS_DEV + block_orders(key).reshape(-1)


def leaf_of_points(key):
    leaf_ids = jnp.arange(POINTS, dtype=jnp.int32) // LEAF
    return jnp.zeros((POINTS,), jnp.int32).at[input_slots(key)].set(leaf_ids)


def place_points(key, noise, spread):
    depth = NLEAVES.bit_length() - 1
    placed = noise
    for level in range(depth):
        node_total = NLEAVES >> level
        offsets = spread * jnp.clip(jax.random.normal(jax.random.fold_in(key, level), (DIM, node_total), jnp.float32), -4.0, 4.0)
        placed = placed + jnp.repeat(offsets, LEAF << level, axis=1)
    return placed


def shape_state(key, noise, means, leaf_ids, rise):
    rhs_scale = jnp.exp(jax.random.uniform(jax.random.fold_in(key, 3), (NRHS, 1), jnp.float32, math.log(0.2), math.log(2.0)))
    device_pos = (jnp.arange(POINTS, dtype=jnp.int32) // PTS_DEV).astype(jnp.float32)
    device_scale = rise ** (device_pos / (N_LEAF - 1))
    return (noise + means[:, leaf_ids]) * rhs_scale * device_scale[None, :]


def draw_order(key, part):
    return block_orders(key).reshape(-1)


def draw_coords(key, part):
    slots = input_slots(key)
    key = jax.random.fold_in(key, 7)
    noise = 1.7 * jnp.clip(jax.random.normal(jax.random.fold_in(key, 1000), (DIM, POINTS), jnp.float32), -4.0, 4.0)
    placed = place_points(key, noise, 0.8)
    return jnp.zeros((DIM, POINTS), jnp.float32).at[:, slots].set(placed)


def draw_residual(key, part):
    leaf_ids = leaf_of_points(key)
    key = jax.random.fold_in(key, 11)
    noise = jnp.clip(jax.random.normal(jax.random.fold_in(key, 1), (NRHS, POINTS), jnp.float32), -4.0, 4.0)
    means = jnp.clip(jax.random.normal(jax.random.fold_in(key, 2), (NRHS, NLEAVES), jnp.float32), -3.0, 3.0)
    return shape_state(key, noise, means, leaf_ids, 3.0)


def draw_direction(key, part):
    leaf_ids = leaf_of_points(key)
    key = jax.random.fold_in(key, 13)
    noise = jnp.clip(jax.random.normal(jax.random.fold_in(key, 1), (NRHS, POINTS), jnp.float32), -4.0, 4.0)
    means = jnp.clip(jax.random.normal(jax.random.fold_in(key, 2), (NRHS, NLEAVES), jnp.float32), -3.0, 3.0)
    return shape_state(key, noise, means, leaf_ids, 3.0)


def draw_leaf_skel(key, part):
    key = jax.random.fold_in(key, 21)
    keys = jax.random.split(key, NLEAVES)
    return jax.vmap(lambda sub_key: jax.random.permutation(sub_key, LEAF)[:RANK])(keys).astype(jnp.int32)


def draw_local_skel(key, part):
    key = jax.random.fold_in(key, 23)
    keys = jax.random.split(key, N_LEAF * (LEAVES_DEV - 1))
    return jax.vmap(lambda sub_key: jax.random.permutation(sub_key, 2 * RANK)[:RANK])(keys).astype(jnp.int32)


def draw_upper_skel(key, part):
    key = jax.random.fold_in(key, 29)
    layers = []
    for level in range(ULEV):
        node_total = N_LEAF >> level + 1
        keys = jax.random.split(jax.random.fold_in(key, level), node_total)
        table = jax.vmap(lambda sub_key: jax.random.permutation(sub_key, 2 * RANK)[:RANK])(keys)
        layers.append(jnp.repeat(table, 2 ** (level + 1), axis=0))
    return jnp.stack(layers).astype(jnp.int32)


def levels(rng, dims, cuts, low, largest):
    def one(position, parts):
        steps = jax.random.uniform(jax.random.fold_in(jax.random.fold_in(rng, 6), position), (parts,), jnp.float32, low / len(cuts), largest / len(cuts))
        return jnp.repeat(jnp.exp(steps), dims[position] // parts).reshape((-1,) + (1,) * (len(dims) - position - 1))

    level = one(*cuts[0])
    for cut in cuts[1:]:
        level = level * one(*cut)
    return level


def normal_values(key, extent, scale, reach, pieces=(), kind=jnp.bfloat16):
    level = levels(key, extent, pieces, -0.22, 0.18) if pieces else 1.0
    array = jax.random.normal(key, extent, jnp.float32) * scale * level
    return jnp.minimum(jnp.maximum(array, -reach), reach).astype(kind)


def setup_inputs(seed: int = 0) -> dict:
    key_list = jax.random.split(jax.random.key(seed), 9)
    coords = draw_coords(jax.random.fold_in(key_list[8], 71), 0)
    solution = normal_values(key_list[1], (NRHS, POINTS), 1.0, 6.0, ((1, 256),), jnp.float32)
    residual = draw_residual(jax.random.fold_in(key_list[8], 71), 0)
    direction = draw_direction(jax.random.fold_in(key_list[8], 71), 0)
    order = draw_order(jax.random.fold_in(key_list[8], 71), 0)
    leaf_skel = draw_leaf_skel(jax.random.fold_in(key_list[8], 71), 0)
    local_skel = draw_local_skel(jax.random.fold_in(key_list[8], 71), 0)
    upper_skel = draw_upper_skel(jax.random.fold_in(key_list[8], 71), 0)
    return {"coords": coords, "solution": solution, "residual": residual, "direction": direction, "order": order, "leaf_skel": leaf_skel, "local_skel": local_skel, "upper_skel": upper_skel}


ridge = 0.5
exact = lax.Precision.HIGHEST


def pair_scores(left_pts, right_pts):
    cross_term = jnp.einsum("...dn,...dm->...nm", left_pts, right_pts, precision=exact)
    left_sq = jnp.sum(left_pts * left_pts, axis=-2)
    right_sq = jnp.sum(right_pts * right_pts, axis=-2)
    dim_count = left_pts.shape[-2]
    return -(left_sq[..., :, None] + right_sq[..., None, :] - 2.0 * cross_term) / (2.0 * dim_count)


def interpolate(points, skeleton):
    return jax.nn.softmax(pair_scores(points, skeleton), axis=-1)


def kernel_block(left_pts, right_pts, leaf_size):
    return jnp.exp(pair_scores(left_pts, right_pts)) / leaf_size


def select_columns(blocks, index_list):
    return jnp.take_along_axis(blocks, index_list[:, None, :], axis=2)


def join_pairs(skeletons):
    node_count, dim_count, rank_size = skeletons.shape
    paired = skeletons.reshape(node_count // 2, 2, dim_count, rank_size).transpose(0, 2, 1, 3)
    return paired.reshape(node_count // 2, dim_count, 2 * rank_size)


def sibling_terms(values, couplings):
    first_half = jnp.einsum("ijb,iab->ija", values[1::2], couplings, precision=exact)
    second_half = jnp.einsum("ija,iab->ijb", values[0::2], couplings, precision=exact)
    return jnp.stack([first_half, second_half], axis=1).reshape(values.shape)


def node_lists(local_skel, upper_skel):
    per_device = local_skel.reshape(N_LEAF, LEAVES_DEV - 1, RANK)
    lists = []
    offset = 0
    width_now = LEAVES_DEV // 2
    while width_now >= 1:
        lists.append(per_device[:, offset:offset + width_now].reshape(-1, RANK))
        offset += width_now
        width_now //= 2
    for level in range(ULEV):
        lists.append(upper_skel[level, :: 2 ** (level + 1)])
    return lists


def build_tree(points, leaf_skel, lists):
    leaf_points = points.reshape(DIM, NLEAVES, LEAF).transpose(1, 0, 2)
    skeleton = select_columns(leaf_points, leaf_skel)
    leaf_skeleton = skeleton
    transfers = []
    couplings = []
    for index_list in lists:
        parent = select_columns(join_pairs(skeleton), index_list)
        transfers.append(interpolate(skeleton, jnp.repeat(parent, 2, axis=0)))
        couplings.append(kernel_block(skeleton[0::2], skeleton[1::2], LEAF))
        skeleton = parent
    couplings.append(kernel_block(skeleton[0::2], skeleton[1::2], LEAF))
    return leaf_points, leaf_skeleton, transfers, couplings


def apply_operator(vectors, leaf_points, leaf_skeleton, transfers, couplings):
    blocks = vectors.reshape(NRHS, NLEAVES, LEAF).transpose(1, 0, 2)

    def leaf_upward(item):
        block_pts, block_skel, block_vec = item
        near_part = jnp.dot(block_vec, kernel_block(block_pts, block_pts, LEAF), precision=exact)
        coarse = jnp.dot(block_vec, interpolate(block_pts, block_skel), precision=exact)
        return near_part, coarse

    near_parts, coarse = lax.map(leaf_upward, (leaf_points, leaf_skeleton, blocks))
    upward = [coarse]
    for transfer in transfers:
        moved = jnp.einsum("cjr,crs->cjs", upward[-1], transfer, precision=exact)
        upward.append(moved[0::2] + moved[1::2])
    downward = sibling_terms(upward[-1], couplings[-1])
    for level in range(len(couplings) - 2, -1, -1):
        carried = jnp.einsum("cjs,crs->cjr", jnp.repeat(downward, 2, axis=0), transfers[level], precision=exact)
        downward = sibling_terms(upward[level], couplings[level]) + carried

    def leaf_downward(item):
        block_pts, block_skel, block_coarse, block_near = item
        basis = interpolate(block_pts, block_skel)
        return block_near + jnp.einsum("jr,qr->jq", block_coarse, basis, precision=exact)

    result = lax.map(leaf_downward, (leaf_points, leaf_skeleton, downward, near_parts))
    return ridge * vectors + result.transpose(1, 0, 2).reshape(NRHS, POINTS)


def reference(coords, solution, residual, direction, order, leaf_skel, local_skel, upper_skel):
    positions = jnp.arange(POINTS, dtype=jnp.int32)
    index_map = (positions // PTS_DEV) * PTS_DEV + order.astype(jnp.int32)
    inverse = jnp.zeros((POINTS,), jnp.int32).at[index_map].set(positions)
    points = coords[:, index_map]
    leaf_points, leaf_skeleton, transfers, couplings = build_tree(points, leaf_skel, node_lists(local_skel, upper_skel))
    iterate = solution[:, index_map]
    resid = residual[:, index_map]
    search = direction[:, index_map]
    norm_now = jnp.sum(resid * resid, axis=1)
    for step_index in range(ITERS):
        image = apply_operator(search, leaf_points, leaf_skeleton, transfers, couplings)
        step_size = norm_now / jnp.sum(search * image, axis=1)
        iterate = iterate + step_size[:, None] * search
        resid = resid - step_size[:, None] * image
        norm_next = jnp.sum(resid * resid, axis=1)
        search = resid + (norm_next / norm_now)[:, None] * search
        norm_now = norm_next
    return iterate[:, inverse], resid[:, inverse], search[:, inverse]
```

```python
import math

import jax
import jax.numpy as jnp
from jax import lax
from jax.experimental import pallas as pl
from jax.experimental.pallas import tpu as pltpu
from jax.sharding import PartitionSpec as P

ITERS = 4
MESH = pl.DeviceIdType.MESH
LANES = 128
LOG2E = math.log2(math.e)
F32 = jnp.float32
BF16 = jnp.bfloat16
VMEM = pl.BlockSpec(memory_space=pltpu.VMEM)

OWN0, OWN1, OWN2, OWN3, UP0, UP1, SIB, COUSIN, UNCLE, DOWN0, DOWN1 = range(11)
PER_ROUND = 11


def pick(sources, index_row, first_block, block_count):
    low = index_row & (LANES - 1)
    high = index_row >> 7
    outs = [None] * len(sources)
    for block in range(block_count):
        hit = None
        for n, source in enumerate(sources):
            held = source(first_block + block)
            rows = held.shape[0]
            place = jnp.broadcast_to(low, (rows, LANES))
            got = jnp.take_along_axis(held, place, axis=1, mode="promise_in_bounds")
            if outs[n] is None:
                outs[n] = got
            else:
                hit = jnp.broadcast_to(high, (rows, LANES)) == block
                outs[n] = jnp.where(hit, got, outs[n])
    return outs


def block_of(ref):
    return lambda b: ref[:, b * LANES : (b + 1) * LANES]


def arrange(coords, resid, search, order, leaf_skel, local_skel, pts, r_out, p_out, inverse, skel, parent, digits, marks):
    blocks = order.shape[0]
    sources = [block_of(coords), block_of(resid), block_of(search)]

    def body(ob, carry):
        row = order[pl.ds(ob, 1), :]
        got = pick(sources, row, 0, blocks)
        span = pl.ds(pl.multiple_of(ob * LANES, LANES), LANES)
        for ref, value in zip((pts, r_out, p_out), got):
            ref[:, span] = value
        place = ob * LANES + lax.broadcasted_iota(jnp.int32, (blocks, LANES), 1)
        hit = lax.broadcasted_iota(jnp.int32, (blocks, LANES), 0) == (row >> 7)
        coarse = jnp.where(hit, (place >> 5).astype(F32), 0.0)
        fine = jnp.where(hit, (place & 31).astype(F32), 0.0)
        digits[0:blocks, span] = coarse.astype(BF16)
        digits[blocks : 2 * blocks, span] = fine.astype(BF16)
        lane_hit = lax.broadcasted_iota(jnp.int32, (LANES, LANES), 0) == (row & (LANES - 1))
        marks[:, span] = jnp.where(lane_hit, 1.0, 0.0).astype(BF16)
        return carry

    lax.fori_loop(0, blocks, body, 0)
    found = lax.dot_general(digits[...], marks[...], (((1,), (1,)), ((), ())), preferred_element_type=F32)
    inverse[...] = (found[0:blocks] * 32.0 + found[blocks : 2 * blocks]).astype(jnp.int32)
    leaves = skel.shape[0]
    rank = leaf_skel.shape[1]
    leaf_blocks = blocks // leaves
    for leaf in range(leaves):
        for ob in range(rank // LANES):
            row = leaf_skel[leaf : leaf + 1, ob * LANES : (ob + 1) * LANES]
            (got,) = pick([block_of(pts)], row, leaf * leaf_blocks, leaf_blocks)
            skel[leaf, :, ob * LANES : (ob + 1) * LANES] = got
    per = rank // LANES
    both = lambda b: skel[b // per, :, (b % per) * LANES : (b % per + 1) * LANES]
    for ob in range(per):
        row = local_skel[0:1, ob * LANES : (ob + 1) * LANES]
        (got,) = pick([both], row, 0, 2 * per)
        parent[:, ob * LANES : (ob + 1) * LANES] = got


def restore(x_in, gain, resid, search, inverse, x_out, r_out, p_out):
    blocks = inverse.shape[0]
    sources = [block_of(gain), block_of(resid), block_of(search)]

    def body(ob, carry):
        row = inverse[pl.ds(ob, 1), :]
        span = pl.ds(pl.multiple_of(ob * LANES, LANES), LANES)
        got = pick(sources, row, 0, blocks)
        x_out[:, span] = x_in[:, span] + got[0]
        r_out[:, span] = got[1]
        p_out[:, span] = got[2]
        return carry

    lax.fori_loop(0, blocks, body, 0)


def split(value):
    high = value.astype(BF16)
    return high, (value - high.astype(F32)).astype(BF16)


def split3(value):
    high = value.astype(BF16)
    rest = value - high.astype(F32)
    mid = rest.astype(BF16)
    return high, mid, (rest - mid.astype(F32)).astype(BF16)


def mm(a, b):
    return jnp.dot(a, b, preferred_element_type=F32)


def norm_rows(norms, first):
    high, mid, low = (part.astype(F32) for part in split3(norms))
    shape = (16, norms.shape[1])
    row = lax.broadcasted_iota(jnp.int32, shape, 0)
    one = jnp.where((row >= 3 - first) & (row < 6 - first), 1.0, 0.0)
    tile = jnp.where(row == first, high, one)
    tile = jnp.where(row == first + 1, mid, tile)
    return jnp.where(row == first + 2, low, tile)


def left_form(points):
    high, mid, low = (part.astype(F32) for part in split3(points))
    norms = jnp.sum(points * points, axis=0, keepdims=True) * (-LOG2E / 32.0)
    extra = norm_rows(norms, 0)
    full = jnp.concatenate([high, high, mid, mid, high, low, extra, jnp.zeros_like(extra)], axis=0)
    return jnp.transpose(full, (1, 0)).astype(BF16)


def right_form(points):
    high, mid, low = split3(points * (LOG2E / 16.0))
    norms = jnp.sum(points * points, axis=0, keepdims=True) * (-LOG2E / 32.0)
    extra = norm_rows(norms, 3).astype(BF16)
    return jnp.concatenate([high, mid, high, mid, low, high, extra, jnp.zeros_like(extra)], axis=0)


def softmax2(scores, axis):
    weights = jnp.exp2(scores - jnp.max(scores, axis=axis, keepdims=True))
    return weights / jnp.sum(weights, axis=axis, keepdims=True)


def row_dot(a, b):
    return jnp.sum(a * b, axis=1, keepdims=True)


def solve(pts, r_in, p_in, skel0, skel1, upper, gain, r_out, p_out,
          near_mat, uq_hi, uq_lo, ut_hi, ut_lo, t_hi, t_lo, vec, vsplit, image, q_ref,
          state, points_out, points_in, coef_out, coef_in, sum_out, sum_in, cps,
          send_sem, recv_sem):
    me = lax.axis_index("leaf")
    rounds = 4
    leaf_size = near_mat.shape[1]
    leaves = near_mat.shape[0]
    scale = 1.0 / leaf_size
    rank = skel1.shape[1]
    local = rounds * PER_ROUND
    bits = [(me // (1 << u)) % 2 for u in range(2 * rounds)]

    def partner(g, t):
        step = 1 << (2 * g)
        low = (1 - 2 * bits[2 * g]) * step
        high = (1 - 2 * bits[2 * g + 1]) * (2 * step)
        return me + (t % 2) * low + (t // 2) * high

    barrier = pltpu.get_barrier_semaphore()
    for g in range(rounds):
        for t in range(1, 4):
            pl.semaphore_signal(barrier, inc=1, device_id=(partner(g, t),), device_id_type=MESH)
    pl.semaphore_wait(barrier, 3 * rounds)

    def copies(src, dst, phase, g):
        return [
            pltpu.make_async_remote_copy(
                src_ref=src,
                dst_ref=dst.at[t - 1],
                send_sem=send_sem.at[g, t - 1],
                recv_sem=recv_sem.at[phase, g, t - 1],
                device_id=(partner(g, t),),
                device_id_type=MESH,
            )
            for t in range(1, 4)
        ]

    def keep(slot, value):
        high, low = split(value)
        t_hi[slot] = high
        t_lo[slot] = low

    def times(value, slot):
        high, low = split(value)
        rows = value.shape[0]
        wide = mm(jnp.concatenate([high, low], axis=0), t_hi[slot])
        return wide[:rows] + wide[rows:] + mm(high, t_lo[slot])

    def choose(first_is_own, index_row, own, other):
        swapped = jnp.where(index_row >= rank, index_row - rank, index_row + rank)
        want = jnp.where(first_is_own, index_row, swapped)
        place = lax.broadcasted_iota(jnp.int32, (rank, rank), 0).astype(F32)
        got = None
        for n, points in enumerate((own, other)):
            hot = jnp.where(place + float(n * rank) == want, 1.0, 0.0).astype(BF16)
            wide = mm(jnp.concatenate(split3(points), axis=0), hot)
            part = (wide[0:16] + wide[16:32]) + wide[32:48]
            got = part if got is None else got + part
        return got

    rows_part = leaf_size // 8

    def near_rows(part):
        leaf = part // 2
        right = right_form(pts[:, leaf * leaf_size : (leaf + 1) * leaf_size])

        def body(j, carry):
            span = pl.ds(pl.multiple_of(((part % 2) * 4 + j) * rows_part, rows_part), rows_part)
            near_mat[leaf, span, :] = jnp.exp2(mm(lefts[leaf, span, :], right)).astype(BF16)
            return carry

        lax.fori_loop(0, 4, body, 0)

    lefts = uq_hi.at[:, :, 0:LANES]
    own = skel1[...]
    for g in range(rounds):
        u = 2 * g
        points_out[g, 0:16, :] = own
        points_out[g, 16:24, :] = jnp.broadcast_to(upper[u : u + 1, :].astype(F32), (8, rank))
        sends = copies(points_out.at[g], points_in.at[g], 0, g)
        for c in sends:
            c.start()
        if g == 0:
            for leaf in range(leaves):
                lefts[leaf] = left_form(pts[:, leaf * leaf_size : (leaf + 1) * leaf_size])
        near_rows(g)
        for c in sends:
            c.wait()
        low = [own] + [points_in[g, t, 0:16, :] for t in range(3)]
        lists = [points_out[g, 16:17, :], points_in[g, 1, 16:17, :]]
        mids = [choose(bits[u] == 0, lists[n], low[2 * n], low[2 * n + 1]) for n in range(2)]
        low_left = [left_form(x) for x in low]
        mid_left = [left_form(x) for x in mids]
        low_right = [right_form(low[0]), None, right_form(low[2])]
        mid_right = [right_form(x) for x in mids]
        base = g * PER_ROUND
        for t in range(4):
            keep(base + OWN0 + t, softmax2(mm(low_left[t], mid_right[t // 2]), 1))
        keep(base + DOWN0, softmax2(mm(mid_left[0], low_right[0]), 0))
        keep(base + SIB, jnp.exp2(mm(low_left[1], low_right[0])) * scale)
        keep(base + COUSIN, jnp.exp2(mm(low_left[3], low_right[2])) * scale)
        keep(base + UNCLE, jnp.exp2(mm(mid_left[1], mid_right[0])) * scale)
        if g + 1 < rounds:
            top = choose(bits[u + 1] == 0, upper[u + 1 : u + 2, :].astype(F32), mids[0], mids[1])
            top_right = right_form(top)
            for n in range(2):
                keep(base + UP0 + n, softmax2(mm(mid_left[n], top_right), 1))
            keep(base + DOWN1, softmax2(mm(left_form(top), mid_right[0]), 0))
            own = top

    skel_left = [left_form(skel0[leaf]) for leaf in range(leaves)]
    skel_right = [right_form(skel0[leaf]) for leaf in range(leaves)]
    parent_left = left_form(skel1[...])
    parent_right = right_form(skel1[...])
    for leaf in range(leaves):
        keep(local + leaf, softmax2(mm(skel_left[leaf], parent_right), 1))
        keep(local + 2 + leaf, softmax2(mm(parent_left, skel_right[leaf]), 0))
        keep(local + 4 + leaf, jnp.exp2(mm(skel_left[1 - leaf], skel_right[leaf])) * scale)

    for leaf in range(leaves):

        def basis_rows(j, carry, leaf=leaf):
            span = pl.ds(pl.multiple_of(j * rank, rank), rank)
            high, low = split(softmax2(mm(lefts[leaf, span, :], skel_right[leaf]), 1))
            uq_lo[leaf, span, :] = low
            uq_hi[leaf, span, :] = high
            return carry

        lax.fori_loop(0, leaf_size // rank, basis_rows, 0)
        right = right_form(pts[:, leaf * leaf_size : (leaf + 1) * leaf_size])
        high, low = split(softmax2(mm(skel_left[leaf], right), 0))
        ut_hi[leaf] = high
        ut_lo[leaf] = low

    vec[...] = p_in[...]
    r_out[...] = r_in[...]
    p_out[...] = jnp.zeros_like(p_out)
    q_ref[...] = jnp.zeros_like(q_ref)
    gain[...] = jnp.zeros_like(gain)
    state[0] = jnp.ones(state.shape[1:], F32)
    state[1] = jnp.zeros(state.shape[1:], F32)
    rhs = vec.shape[0]
    lane = lax.broadcasted_iota(jnp.int32, (rhs, LANES), 1)

    def iteration(k, carry):
        high, low = split(vec[...])
        vsplit[0:rhs, :] = high
        vsplit[rhs : 2 * rhs, :] = low
        fresh = row_dot(r_out[...], r_out[...])
        cross = row_dot(r_out[...], q_ref[...])
        for leaf in range(leaves):

            def near_columns(j, carry, leaf=leaf):
                inner = pl.ds(pl.multiple_of(j * rank, rank), rank)
                span = pl.ds(pl.multiple_of(leaf * leaf_size + j * rank, rank), rank)
                wide = mm(vsplit[:, leaf * leaf_size : (leaf + 1) * leaf_size], near_mat[leaf, :, inner])
                image[:, span] = 0.5 * vec[:, span] + (wide[:rhs] + wide[rhs:]) * scale
                return carry

            lax.fori_loop(0, leaf_size // rank, near_columns, 0)
        total = row_dot(vec[...], image[...])
        leaf_coef = []
        for leaf in range(leaves):
            cols = slice(leaf * leaf_size, (leaf + 1) * leaf_size)
            wide = mm(vsplit[:, cols], uq_hi[leaf])
            leaf_coef.append(wide[:rhs] + wide[rhs:] + mm(vsplit[0:rhs, cols], uq_lo[leaf]))
        coef = times(leaf_coef[0], local) + times(leaf_coef[1], local + 1)
        leaf_cp = [times(leaf_coef[1 - leaf], local + 4 + leaf) for leaf in range(leaves)]
        total = total + 2.0 * row_dot(leaf_coef[0], leaf_cp[0])
        sums = jnp.where(lane == 0, fresh, 0.0)
        sums = jnp.where(lane == 1, cross, sums)
        sums = jnp.where(lane == 2, total, sums)
        for g in range(rounds):
            base = g * PER_ROUND
            coef_out[g, :, 0:rank] = coef
            coef_out[g, :, rank : rank + LANES] = sums
            sends = copies(coef_out.at[g], coef_in.at[k, g], 1 + k, g)
            for c in sends:
                c.start()
            for c in sends:
                c.wait()
            got = [coef] + [coef_in[k, g, t, :, 0:rank] for t in range(3)]
            far = [coef_in[k, g, t, :, rank : rank + LANES] for t in range(3)]
            mid0 = times(got[0], base + OWN0) + times(got[1], base + OWN1)
            mid1 = times(got[2], base + OWN2) + times(got[3], base + OWN3)
            if g + 1 < rounds:
                coef = times(mid0, base + UP0) + times(mid1, base + UP1)
            low_cp = times(got[1], base + SIB)
            mid_cp = times(mid1, base + UNCLE)
            cps[2 * g] = low_cp
            cps[2 * g + 1] = mid_cp
            quad = row_dot(got[0], low_cp) + row_dot(got[2], times(got[3], base + COUSIN)) + row_dot(mid0, mid_cp)
            sums = (sums + far[0]) + (far[1] + far[2]) + jnp.where(lane == 2, 2.0 * quad, 0.0)
        down = cps[2 * rounds - 1]
        for u in range(2 * rounds - 2, -1, -1):
            down = cps[u] + times(down, (u // 2) * PER_ROUND + (DOWN1 if u % 2 else DOWN0))
        for leaf in range(leaves):
            cols = slice(leaf * leaf_size, (leaf + 1) * leaf_size)
            leaf_down = leaf_cp[leaf] + times(down, local + 2 + leaf)
            high, low = split(leaf_down)
            wide = mm(jnp.concatenate([high, low], axis=0), ut_hi[leaf])
            image[:, cols] += wide[:rhs] + wide[rhs:] + mm(high, ut_lo[leaf])
        fresh = sums[:, 0:1]
        cross = sums[:, 1:2]
        beta = fresh / state[0, :, 0:1]
        curve = sums[:, 2:3] + 2.0 * beta * cross + beta * beta * state[1, :, 0:1]
        alpha = fresh / curve
        state[0] = jnp.broadcast_to(fresh, (rhs, LANES))
        state[1] = jnp.broadcast_to(curve, (rhs, LANES))
        p_new = vec[...] + beta * p_out[...]
        q_new = image[...] + beta * q_ref[...]
        p_out[...] = p_new
        q_ref[...] = q_new
        gain[...] += alpha * p_new
        r_new = r_out[...] - alpha * q_new
        r_out[...] = r_new
        vec[...] = r_new
        return carry

    lax.fori_loop(0, ITERS, iteration, 0)
    sums = jnp.broadcast_to(row_dot(r_out[...], r_out[...]), (rhs, LANES))
    for g in range(rounds):
        sum_out[g] = sums
        sends = copies(sum_out.at[g], sum_in.at[g], 1 + ITERS, g)
        for c in sends:
            c.start()
        for c in sends:
            c.wait()
        sums = (sums + sum_in[g, 0]) + (sum_in[g, 1] + sum_in[g, 2])
    beta = sums[:, 0:1] / state[0, :, 0:1]
    p_out[...] = r_out[...] + beta * p_out[...]


def per_device(coords, solution, residual, direction, order, leaf_skel, local_skel, upper_skel):
    dims, count = coords.shape
    rhs = solution.shape[0]
    leaves, rank = leaf_skel.shape
    leaf_size = count // leaves
    blocks = count // LANES
    flat = jax.ShapeDtypeStruct((rhs, count), F32)
    limit = 60 * 1024 * 1024
    pts, resid, search, inverse, skel0, skel1 = pl.pallas_call(
        arrange,
        out_shape=(
            jax.ShapeDtypeStruct((dims, count), F32),
            flat,
            flat,
            jax.ShapeDtypeStruct((blocks, LANES), jnp.int32),
            jax.ShapeDtypeStruct((leaves, dims, rank), F32),
            jax.ShapeDtypeStruct((dims, rank), F32),
        ),
        in_specs=[VMEM] * 6,
        out_specs=(VMEM,) * 6,
        scratch_shapes=[pltpu.VMEM((2 * blocks, count), BF16), pltpu.VMEM((LANES, count), BF16)],
        compiler_params=pltpu.CompilerParams(vmem_limit_bytes=limit),
    )(coords, residual, direction, order.reshape(blocks, LANES), leaf_skel, local_skel)
    slots = 4 * PER_ROUND + 6
    gain, resid, search = pl.pallas_call(
        solve,
        out_shape=(flat, flat, flat),
        in_specs=[VMEM] * 6,
        out_specs=(VMEM,) * 3,
        scratch_shapes=[
            pltpu.VMEM((leaves, leaf_size, leaf_size), BF16),
            pltpu.VMEM((leaves, leaf_size, rank), BF16),
            pltpu.VMEM((leaves, leaf_size, rank), BF16),
            pltpu.VMEM((leaves, rank, leaf_size), BF16),
            pltpu.VMEM((leaves, rank, leaf_size), BF16),
            pltpu.VMEM((slots, rank, rank), BF16),
            pltpu.VMEM((slots, rank, rank), BF16),
            pltpu.VMEM((rhs, count), F32),
            pltpu.VMEM((2 * rhs, count), BF16),
            pltpu.VMEM((rhs, count), F32),
            pltpu.VMEM((rhs, count), F32),
            pltpu.VMEM((2, rhs, LANES), F32),
            pltpu.VMEM((4, dims + 8, rank), F32),
            pltpu.VMEM((4, 3, dims + 8, rank), F32),
            pltpu.VMEM((4, rhs, rank + LANES), F32),
            pltpu.VMEM((ITERS, 4, 3, rhs, rank + LANES), F32),
            pltpu.VMEM((4, rhs, LANES), F32),
            pltpu.VMEM((4, 3, rhs, LANES), F32),
            pltpu.VMEM((8, rhs, rank), F32),
            pltpu.SemaphoreType.DMA((4, 3)),
            pltpu.SemaphoreType.DMA((ITERS + 2, 4, 3)),
        ],
        compiler_params=pltpu.CompilerParams(vmem_limit_bytes=limit, collective_id=0, has_side_effects=True),
    )(pts, resid, search, skel0, skel1, upper_skel.reshape(-1, rank))
    return pl.pallas_call(
        restore,
        out_shape=(flat, flat, flat),
        in_specs=[VMEM] * 5,
        out_specs=(VMEM,) * 3,
        compiler_params=pltpu.CompilerParams(vmem_limit_bytes=limit),
    )(solution, gain, resid, search, inverse)


def solution(mesh):
    in_specs = (
        P(None, "leaf"),
        P(None, "leaf"),
        P(None, "leaf"),
        P(None, "leaf"),
        P("leaf"),
        P("leaf", None),
        P("leaf", None),
        P(None, "leaf", None),
    )
    out_specs = (P(None, "leaf"), P(None, "leaf"), P(None, "leaf"))
    return jax.shard_map(
        per_device, mesh=mesh, in_specs=in_specs, out_specs=out_specs, check_vma=False
    )
```

```python
import math

import jax
import jax.numpy as jnp
from jax import lax
from jax.experimental import pallas as pl
from jax.experimental.pallas import tpu as pltpu
from jax.sharding import PartitionSpec as P

ITERS = 4
MESH = pl.DeviceIdType.MESH
LANES = 128
LOG2E = math.log2(math.e)
F32 = jnp.float32
BF16 = jnp.bfloat16
VMEM = pl.BlockSpec(memory_space=pltpu.VMEM)

OWN0, OWN1, OWN2, OWN3, UP0, UP1, SIB, COUSIN, UNCLE = range(9)
PER_ROUND = 9


def pick(sources, index_row, first_block, block_count):
    low = index_row & (LANES - 1)
    high = index_row >> 7
    outs = [None] * len(sources)
    for block in range(block_count):
        hit = None
        for n, source in enumerate(sources):
            held = source(first_block + block)
            rows = held.shape[0]
            place = jnp.broadcast_to(low, (rows, LANES))
            got = jnp.take_along_axis(held, place, axis=1, mode="promise_in_bounds")
            if outs[n] is None:
                outs[n] = got
            else:
                hit = jnp.broadcast_to(high, (rows, LANES)) == block
                outs[n] = jnp.where(hit, got, outs[n])
    return outs


def block_of(ref):
    return lambda b: ref[:, b * LANES : (b + 1) * LANES]


def split(value):
    high = value.astype(BF16)
    return high, (value - high.astype(F32)).astype(BF16)


def split3(value):
    high = value.astype(BF16)
    rest = value - high.astype(F32)
    mid = rest.astype(BF16)
    return high, mid, (rest - mid.astype(F32)).astype(BF16)


def mm(a, b):
    return jnp.dot(a, b, preferred_element_type=F32)


def mm_t(a, b):
    return lax.dot_general(a, b, (((1,), (1,)), ((), ())), preferred_element_type=F32)


def stack3(value):
    return jnp.concatenate(split3(value), axis=0)


def fold3(wide):
    rows = wide.shape[0] // 3
    return wide[:rows] + (wide[rows : 2 * rows] + wide[2 * rows :])


def norm_rows(norms, first):
    high, mid, low = (part.astype(F32) for part in split3(norms))
    shape = (16, norms.shape[1])
    row = lax.broadcasted_iota(jnp.int32, shape, 0)
    one = jnp.where((row >= 3 - first) & (row < 6 - first), 1.0, 0.0)
    tile = jnp.where(row == first, high, one)
    tile = jnp.where(row == first + 1, mid, tile)
    return jnp.where(row == first + 2, low, tile)


def left_form(points):
    high, mid, low = (part.astype(F32) for part in split3(points))
    norms = jnp.sum(points * points, axis=0, keepdims=True) * (-LOG2E / 32.0)
    extra = norm_rows(norms, 0)
    full = jnp.concatenate([high, high, mid, mid, high, low, extra, jnp.zeros_like(extra)], axis=0)
    return jnp.transpose(full, (1, 0)).astype(BF16)


def right_form(points):
    high, mid, low = split3(points * (LOG2E / 16.0))
    norms = jnp.sum(points * points, axis=0, keepdims=True) * (-LOG2E / 32.0)
    extra = norm_rows(norms, 3).astype(BF16)
    return jnp.concatenate([high, mid, high, mid, low, high, extra, jnp.zeros_like(extra)], axis=0)


def softmax2(scores, axis):
    weights = jnp.exp2(scores - jnp.max(scores, axis=axis, keepdims=True))
    return weights * (1.0 / jnp.sum(weights, axis=axis, keepdims=True))


def row_dot(a, b):
    return jnp.sum(a * b, axis=1, keepdims=True)


def solve(coords, x_in, r_in, p_in, order, leaf_skel, local_skel, upper, x_out, r_out, p_out,
          near_mat, lefts, rights, ut_hi, ut_lo, t_hi, t_lo, pts, vec, vsplit, image, q_ref, r_ref, p_ref, gain,
          digits, marks, inverse, skel, parent, state, cps,
          points_out, points_in, coef_out, coef_in, line_out, line_in, sum_out, sum_in,
          send_sem, recv_sem, line_send, line_recv):
    me = lax.axis_index("leaf")
    rounds = 4
    line = 16
    leaves, leaf_size = near_mat.shape[0], near_mat.shape[1]
    scale = 1.0 / leaf_size
    rank = parent.shape[1]
    rhs = vec.shape[0]
    local = rounds * PER_ROUND
    blocks = order.shape[0]
    bits = [(me // (1 << u)) % 2 for u in range(2 * rounds)]

    def partner(g, t):
        step = 1 << (2 * g)
        low = (1 - 2 * bits[2 * g]) * step
        high = (1 - 2 * bits[2 * g + 1]) * (2 * step)
        return me + (t % 2) * low + (t // 2) * high

    def on_line(t):
        return me + sum((1 - 2 * bits[u]) * (1 << u) for u in range(4) if t >> u & 1)

    barrier = pltpu.get_barrier_semaphore()
    for t in range(1, line):
        pl.semaphore_signal(barrier, inc=1, device_id=(on_line(t),), device_id_type=MESH)
    for g in range(2, rounds):
        for t in range(1, 4):
            pl.semaphore_signal(barrier, inc=1, device_id=(partner(g, t),), device_id_type=MESH)

    def copies(src, dst, phase, g):
        return [
            pltpu.make_async_remote_copy(
                src_ref=src,
                dst_ref=dst.at[t - 1],
                send_sem=send_sem.at[g, t - 1],
                recv_sem=recv_sem.at[phase, g, t - 1],
                device_id=(partner(g, t),),
                device_id_type=MESH,
            )
            for t in range(1, 4)
        ]

    def line_copies(phase):
        return [
            pltpu.make_async_remote_copy(
                src_ref=line_out,
                dst_ref=line_in.at[phase, t - 1],
                send_sem=line_send.at[t - 1],
                recv_sem=line_recv.at[phase, t - 1],
                device_id=(on_line(t),),
                device_id_type=MESH,
            )
            for t in range(1, line)
        ]

    tile_lane = lax.broadcasted_iota(jnp.int32, (8, LANES), 1)

    def to_tile(column):
        return jnp.where(tile_lane == 0, column[0:8], jnp.where(tile_lane == 1, column[8:16], 0.0))

    def from_tile(tile):
        return jnp.concatenate([tile[:, 0:1], tile[:, 1:2]], axis=0)

    def line_sum(phase):
        parts = [line_out[...]] + [line_in[phase, t] for t in range(line - 1)]
        while len(parts) > 1:
            parts = [a + b for a, b in zip(parts[0::2], parts[1::2])]
        return parts[0]

    def keep(slot, value):
        high, low = split(value)
        t_hi[slot] = high
        t_lo[slot] = low

    def times(stacked, slot):
        return fold3(mm(stacked, t_hi[slot]) + mm(stacked, t_lo[slot]))

    def times_t(stacked, slot):
        return fold3(mm_t(stacked, t_hi[slot]) + mm_t(stacked, t_lo[slot]))

    def choose(first_is_own, index_row, own, other):
        swapped = jnp.where(index_row >= rank, index_row - rank, index_row + rank)
        want = jnp.where(first_is_own, index_row, swapped)
        place = lax.broadcasted_iota(jnp.int32, (rank, rank), 0).astype(F32)
        got = None
        for n, points in enumerate((own, other)):
            hot = jnp.where(place + float(n * rank) == want, 1.0, 0.0).astype(BF16)
            part = fold3(mm(stack3(points), hot))
            got = part if got is None else got + part
        return got

    def place_points(ob, carry):
        row = order[pl.ds(ob, 1), :]
        span = pl.ds(pl.multiple_of(ob * LANES, LANES), LANES)
        pts[:, span] = pick([block_of(coords)], row, 0, blocks)[0]
        place = ob * LANES + lax.broadcasted_iota(jnp.int32, (blocks, LANES), 1)
        hit = lax.broadcasted_iota(jnp.int32, (blocks, LANES), 0) == (row >> 7)
        digits[0:blocks, span] = jnp.where(hit, (place >> 5).astype(F32), 0.0).astype(BF16)
        digits[blocks : 2 * blocks, span] = jnp.where(hit, (place & 31).astype(F32), 0.0).astype(BF16)
        lane_hit = lax.broadcasted_iota(jnp.int32, (LANES, LANES), 0) == (row & (LANES - 1))
        marks[:, span] = jnp.where(lane_hit, 1.0, 0.0).astype(BF16)
        return carry

    lax.fori_loop(0, blocks, place_points, 0)
    leaf_blocks = blocks // leaves
    per = rank // LANES
    for leaf in range(leaves):
        for ob in range(per):
            row = leaf_skel[leaf : leaf + 1, ob * LANES : (ob + 1) * LANES]
            (got,) = pick([block_of(pts)], row, leaf * leaf_blocks, leaf_blocks)
            skel[leaf, :, ob * LANES : (ob + 1) * LANES] = got
    both = lambda b: skel[b // per, :, (b % per) * LANES : (b % per + 1) * LANES]
    for ob in range(per):
        row = local_skel[0:1, ob * LANES : (ob + 1) * LANES]
        (got,) = pick([both], row, 0, 2 * per)
        parent[:, ob * LANES : (ob + 1) * LANES] = got
    pl.semaphore_wait(barrier, line - 1 + 3 * (rounds - 2))

    def place_state():
        sources = [block_of(r_in), block_of(p_in)]

        def body(ob, carry):
            span = pl.ds(pl.multiple_of(ob * LANES, LANES), LANES)
            got = pick(sources, order[pl.ds(ob, 1), :], 0, blocks)
            r_ref[:, span] = got[0]
            vec[:, span] = got[1]
            return carry

        lax.fori_loop(0, blocks, body, 0)
        found = mm_t(digits[...], marks[...])
        inverse[...] = (found[0:blocks] * 32.0 + found[blocks : 2 * blocks]).astype(jnp.int32)

    def make_near():
        for leaf in range(leaves):
            cols = slice(leaf * leaf_size, (leaf + 1) * leaf_size)
            lefts[leaf] = left_form(pts[:, cols])
            rights[:, cols] = right_form(pts[:, cols])

            def body(j, carry, leaf=leaf, cols=cols):
                span = pl.ds(pl.multiple_of(j * rank, rank), rank)
                near_mat[leaf, span, :] = jnp.exp2(mm(lefts[leaf, span, :], rights[:, cols])).astype(BF16)
                return carry

            lax.fori_loop(0, leaf_size // rank, body, 0)

    def make_basis(leaf):
        left = left_form(skel[leaf])

        def body(j, carry):
            inner = pl.ds(pl.multiple_of(j * rank, rank), rank)
            span = pl.ds(pl.multiple_of(leaf * leaf_size + j * rank, rank), rank)
            high, low = split(softmax2(mm(left, rights[:, span]), 0))
            ut_hi[leaf, :, inner] = high
            ut_lo[leaf, :, inner] = low
            return carry

        lax.fori_loop(0, leaf_size // rank, body, 0)

    def make_local():
        skel_left = [left_form(skel[leaf]) for leaf in range(leaves)]
        parent_right = right_form(parent[...])
        for leaf in range(leaves):
            keep(local + leaf, softmax2(mm(skel_left[leaf], parent_right), 1))
        keep(local + 2, jnp.exp2(mm(skel_left[0], right_form(skel[1]))) * scale)

    beside = [place_state, make_near, lambda: make_basis(0), lambda: make_basis(1)]
    later = make_local
    own = parent[...]
    for g in range(rounds):
        u = 2 * g
        points_out[g, 0:16, :] = own
        points_out[g, 16:24, :] = jnp.broadcast_to(upper[u : u + 1, :].astype(F32), (8, rank))
        sends = copies(points_out.at[g], points_in.at[g], 0, g)
        for c in sends:
            c.start()
        later()
        beside[g]()
        for c in sends:
            c.wait()
        low = [own] + [points_in[g, t, 0:16, :] for t in range(3)]
        lists = [points_out[g, 16:17, :], points_in[g, 1, 16:17, :]]
        mids = [choose(bits[u] == 0, lists[n], low[2 * n], low[2 * n + 1]) for n in range(2)]
        top = None
        if g + 1 < rounds:
            top = choose(bits[u + 1] == 0, upper[u + 1 : u + 2, :].astype(F32), mids[0], mids[1])

        def later(base=g * PER_ROUND, low=low, mids=mids, top=top):
            low_left = [left_form(x) for x in low]
            mid_left = [left_form(x) for x in mids]
            mid_right = [right_form(x) for x in mids]
            for t in range(4):
                keep(base + OWN0 + t, softmax2(mm(low_left[t], mid_right[t // 2]), 1))
            keep(base + SIB, jnp.exp2(mm(low_left[1], right_form(low[0]))) * scale)
            keep(base + COUSIN, jnp.exp2(mm(low_left[3], right_form(low[2]))) * scale)
            keep(base + UNCLE, jnp.exp2(mm(mid_left[1], mid_right[0])) * scale)
            if top is not None:
                top_right = right_form(top)
                for n in range(2):
                    keep(base + UP0 + n, softmax2(mm(mid_left[n], top_right), 1))

        own = top
    later()

    p_ref[...] = jnp.zeros_like(p_ref)
    q_ref[...] = jnp.zeros_like(q_ref)
    gain[...] = jnp.zeros_like(gain)
    state[0] = jnp.ones(state.shape[1:], F32)
    state[1] = jnp.zeros(state.shape[1:], F32)
    lane = lax.broadcasted_iota(jnp.int32, (rhs, LANES), 1)

    def near_product(leaf):
        def body(j, carry):
            inner = pl.ds(pl.multiple_of(j * rank, rank), rank)
            span = pl.ds(pl.multiple_of(leaf * leaf_size + j * rank, rank), rank)
            wide = fold3(mm(vsplit[:, leaf * leaf_size : (leaf + 1) * leaf_size], near_mat[leaf, :, inner]))
            image[:, span] = 0.5 * vec[:, span] + wide * scale
            return carry

        lax.fori_loop(0, leaf_size // rank, body, 0)

    def iteration(k, carry):
        vsplit[...] = stack3(vec[...])
        leaf_coef = []
        for leaf in range(leaves):
            part = vsplit[:, leaf * leaf_size : (leaf + 1) * leaf_size]
            leaf_coef.append(fold3(mm_t(part, ut_hi[leaf]) + mm_t(part, ut_lo[leaf])))
        wide = [stack3(x) for x in leaf_coef]
        coef = times(wide[0], local) + times(wide[1], local + 1)
        leaf_cp = [times_t(wide[1], local + 2), times(wide[0], local + 2)]
        sums = jnp.where(lane == 0, row_dot(r_ref[...], r_ref[...]), 0.0)
        sums = jnp.where(lane == 1, row_dot(r_ref[...], q_ref[...]), sums)
        sums = jnp.where(lane == 2, 2.0 * row_dot(leaf_coef[0], leaf_cp[0]), sums)
        for g in range(rounds):
            base = g * PER_ROUND
            if g == 2:
                sums = jnp.where(lane == 3, row_dot(vec[...], image[...]), sums)
            coef_out[g, :, 0:rank] = coef
            coef_out[g, :, rank : rank + LANES] = sums
            sends = copies(coef_out.at[g], coef_in.at[k, g], 1 + k, g)
            for c in sends:
                c.start()
            if g < leaves:
                near_product(g)
            for c in sends:
                c.wait()
            got = [coef] + [coef_in[k, g, t, :, 0:rank] for t in range(3)]
            far = [coef_in[k, g, t, :, rank : rank + LANES] for t in range(3)]
            wide = [stack3(x) for x in got]
            mid0 = times(wide[0], base + OWN0) + times(wide[1], base + OWN1)
            mid1 = times(wide[2], base + OWN2) + times(wide[3], base + OWN3)
            mid1_wide = stack3(mid1)
            if g + 1 < rounds:
                coef = times(stack3(mid0), base + UP0) + times(mid1_wide, base + UP1)
            low_cp = times(wide[1], base + SIB)
            mid_cp = times(mid1_wide, base + UNCLE)
            cps[2 * g] = low_cp
            cps[2 * g + 1] = mid_cp
            quad = row_dot(got[0], low_cp) + row_dot(got[2], times(wide[3], base + COUSIN)) + row_dot(mid0, mid_cp)
            sums = (sums + far[0]) + (far[1] + far[2]) + jnp.where(lane == 2, 2.0 * quad, 0.0)
        line_out[...] = to_tile(sums[:, 3:4])
        sends = line_copies(k)
        for c in sends:
            c.start()
        down = cps[2 * rounds - 1]
        for u in range(2 * rounds - 2, -1, -1):
            down = cps[u] + times_t(stack3(down), (u // 2) * PER_ROUND + (UP0 if u % 2 else OWN0))
        down_wide = stack3(down)
        for leaf in range(leaves):
            cols = slice(leaf * leaf_size, (leaf + 1) * leaf_size)
            part = stack3(leaf_cp[leaf] + times_t(down_wide, local + leaf))
            image[:, cols] += fold3(mm(part, ut_hi[leaf]) + mm(part, ut_lo[leaf]))
        for c in sends:
            c.wait()
        near = from_tile(line_sum(k))
        fresh = sums[:, 0:1]
        cross = sums[:, 1:2]
        beta = fresh / state[0, :, 0:1]
        curve = (sums[:, 2:3] + near) + 2.0 * beta * cross + beta * beta * state[1, :, 0:1]
        alpha = fresh / curve
        state[0] = jnp.broadcast_to(fresh, (rhs, LANES))
        state[1] = jnp.broadcast_to(curve, (rhs, LANES))
        p_new = vec[...] + beta * p_ref[...]
        q_new = image[...] + beta * q_ref[...]
        p_ref[...] = p_new
        q_ref[...] = q_new
        gain[...] += alpha * p_new
        r_new = r_ref[...] - alpha * q_new
        r_ref[...] = r_new
        vec[...] = r_new
        return carry

    lax.fori_loop(0, ITERS, iteration, 0)

    sources = [block_of(gain), block_of(r_ref), block_of(p_ref)]

    def restore(ob, carry):
        span = pl.ds(pl.multiple_of(ob * LANES, LANES), LANES)
        got = pick(sources, inverse[pl.ds(ob, 1), :], 0, blocks)
        x_out[:, span] = x_in[:, span] + got[0]
        r_out[:, span] = got[1]
        p_out[:, span] = got[2]
        return carry

    line_out[...] = to_tile(row_dot(r_ref[...], r_ref[...]))
    sends = line_copies(ITERS)
    for c in sends:
        c.start()
    cut = [0, blocks * 7 // 16, blocks * 23 // 32, blocks]
    lax.fori_loop(cut[0], cut[1], restore, 0)
    for c in sends:
        c.wait()
    tile = line_sum(ITERS)
    for g in range(2, rounds):
        sum_out[g - 2] = tile
        sends = copies(sum_out.at[g - 2], sum_in.at[g - 2], 1 + ITERS, g)
        for c in sends:
            c.start()
        lax.fori_loop(cut[g - 1], cut[g], restore, 0)
        for c in sends:
            c.wait()
        tile = (tile + sum_in[g - 2, 0]) + (sum_in[g - 2, 1] + sum_in[g - 2, 2])
    p_out[...] = r_out[...] + from_tile(tile) / state[0, :, 0:1] * p_out[...]


def per_device(coords, solution, residual, direction, order, leaf_skel, local_skel, upper_skel):
    dims, count = coords.shape
    rhs = solution.shape[0]
    leaves, rank = leaf_skel.shape
    leaf_size = count // leaves
    blocks = count // LANES
    flat = jax.ShapeDtypeStruct((rhs, count), F32)
    slots = 4 * PER_ROUND + 3
    return pl.pallas_call(
        solve,
        out_shape=(flat, flat, flat),
        in_specs=[VMEM] * 8,
        out_specs=(VMEM,) * 3,
        scratch_shapes=[
            pltpu.VMEM((leaves, leaf_size, leaf_size), BF16),
            pltpu.VMEM((leaves, leaf_size, LANES), BF16),
            pltpu.VMEM((LANES, count), BF16),
            pltpu.VMEM((leaves, rank, leaf_size), BF16),
            pltpu.VMEM((leaves, rank, leaf_size), BF16),
            pltpu.VMEM((slots, rank, rank), BF16),
            pltpu.VMEM((slots, rank, rank), BF16),
            pltpu.VMEM((dims, count), F32),
            pltpu.VMEM((rhs, count), F32),
            pltpu.VMEM((3 * rhs, count), BF16),
            pltpu.VMEM((rhs, count), F32),
            pltpu.VMEM((rhs, count), F32),
            pltpu.VMEM((rhs, count), F32),
            pltpu.VMEM((rhs, count), F32),
            pltpu.VMEM((rhs, count), F32),
            pltpu.VMEM((2 * blocks, count), BF16),
            pltpu.VMEM((LANES, count), BF16),
            pltpu.VMEM((blocks, LANES), jnp.int32),
            pltpu.VMEM((leaves, dims, rank), F32),
            pltpu.VMEM((dims, rank), F32),
            pltpu.VMEM((2, rhs, LANES), F32),
            pltpu.VMEM((8, rhs, rank), F32),
            pltpu.VMEM((4, dims + 8, rank), F32),
            pltpu.VMEM((4, 3, dims + 8, rank), F32),
            pltpu.VMEM((4, rhs, rank + LANES), F32),
            pltpu.VMEM((ITERS, 4, 3, rhs, rank + LANES), F32),
            pltpu.VMEM((8, LANES), F32),
            pltpu.VMEM((ITERS + 1, 15, 8, LANES), F32),
            pltpu.VMEM((2, 8, LANES), F32),
            pltpu.VMEM((2, 3, 8, LANES), F32),
            pltpu.SemaphoreType.DMA((4, 3)),
            pltpu.SemaphoreType.DMA((ITERS + 2, 4, 3)),
            pltpu.SemaphoreType.DMA((15,)),
            pltpu.SemaphoreType.DMA((ITERS + 1, 15)),
        ],
        compiler_params=pltpu.CompilerParams(
            vmem_limit_bytes=56 * 1024 * 1024, collective_id=0, has_side_effects=True
        ),
    )(
        coords,
        solution,
        residual,
        direction,
        order.reshape(blocks, LANES),
        leaf_skel,
        local_skel,
        jnp.swapaxes(upper_skel, 0, 1).reshape(-1, rank),
    )


def solution(mesh):
    in_specs = (
        P(None, "leaf"),
        P(None, "leaf"),
        P(None, "leaf"),
        P(None, "leaf"),
        P("leaf"),
        P("leaf", None),
        P("leaf", None),
        P(None, "leaf", None),
    )
    out_specs = (P(None, "leaf"), P(None, "leaf"), P(None, "leaf"))
    return jax.shard_map(
        per_device, mesh=mesh, in_specs=in_specs, out_specs=out_specs, check_vma=False
    )
```

```python
import math

import jax
import jax.numpy as jnp
from jax import lax
from jax.experimental import pallas as pl
from jax.experimental.pallas import tpu as pltpu
from jax.sharding import PartitionSpec as P

ITERS = 4
MESH = pl.DeviceIdType.MESH
LANES = 128
LOG2E = math.log2(math.e)
F32 = jnp.float32
BF16 = jnp.bfloat16
VMEM = pl.BlockSpec(memory_space=pltpu.VMEM)

OWN0, OWN1, OWN2, OWN3, UP0, UP1, SIB, COUSIN, UNCLE = range(9)
PER_ROUND = 9


def pick(sources, index_row, first_block, block_count):
    low = index_row & (LANES - 1)
    high = index_row >> 7
    outs = [None] * len(sources)
    for block in range(block_count):
        hit = None
        for n, source in enumerate(sources):
            held = source(first_block + block)
            rows = held.shape[0]
            place = jnp.broadcast_to(low, (rows, LANES))
            got = jnp.take_along_axis(held, place, axis=1, mode="promise_in_bounds")
            if outs[n] is None:
                outs[n] = got
            else:
                hit = jnp.broadcast_to(high, (rows, LANES)) == block
                outs[n] = jnp.where(hit, got, outs[n])
    return outs


def block_of(ref):
    return lambda b: ref[:, b * LANES : (b + 1) * LANES]


def split(value):
    high = value.astype(BF16)
    return high, (value - high.astype(F32)).astype(BF16)


def split3(value):
    high = value.astype(BF16)
    rest = value - high.astype(F32)
    mid = rest.astype(BF16)
    return high, mid, (rest - mid.astype(F32)).astype(BF16)


def mm(a, b):
    return jnp.dot(a, b, preferred_element_type=F32)


def mm_t(a, b):
    return lax.dot_general(a, b, (((1,), (1,)), ((), ())), preferred_element_type=F32)


def stack3(value):
    return jnp.concatenate(split3(value), axis=0)


def fold3(wide):
    rows = wide.shape[0] // 3
    return wide[:rows] + (wide[rows : 2 * rows] + wide[2 * rows :])


def norm_rows(norms, first):
    high, mid, low = (part.astype(F32) for part in split3(norms))
    shape = (16, norms.shape[1])
    row = lax.broadcasted_iota(jnp.int32, shape, 0)
    one = jnp.where((row >= 3 - first) & (row < 6 - first), 1.0, 0.0)
    tile = jnp.where(row == first, high, one)
    tile = jnp.where(row == first + 1, mid, tile)
    return jnp.where(row == first + 2, low, tile)


def left_form(points):
    high, mid, low = (part.astype(F32) for part in split3(points))
    norms = jnp.sum(points * points, axis=0, keepdims=True) * (-LOG2E / 32.0)
    extra = norm_rows(norms, 0)
    full = jnp.concatenate([high, high, mid, mid, high, low, extra, jnp.zeros_like(extra)], axis=0)
    return jnp.transpose(full, (1, 0)).astype(BF16)


def right_form(points):
    high, mid, low = split3(points * (LOG2E / 16.0))
    norms = jnp.sum(points * points, axis=0, keepdims=True) * (-LOG2E / 32.0)
    extra = norm_rows(norms, 3).astype(BF16)
    return jnp.concatenate([high, mid, high, mid, low, high, extra, jnp.zeros_like(extra)], axis=0)


def softmax2(scores, axis):
    weights = jnp.exp2(scores - jnp.max(scores, axis=axis, keepdims=True))
    return weights * (1.0 / jnp.sum(weights, axis=axis, keepdims=True))


def row_dot(a, b):
    return jnp.sum(a * b, axis=1, keepdims=True)


def solve(coords, x_in, r_in, p_in, order, leaf_skel, local_skel, upper, x_out, r_out, p_out,
          near_mat, lefts, rights, ut_hi, ut_lo, t_hi, t_lo, pts, vec, vsplit, image, q_ref, r_ref, p_ref, gain,
          digits, marks, inverse, skel, parent, state, cps,
          points_out, points_in, coef_out, coef_in, sums_out, sums_in, middles, line_out, line_in, plane_in, tile_out, tile_in,
          send_sem, recv_sem, sums_send, sums_recv, line_send, line_recv, plane_recv, tile_send, tile_recv):
    me = lax.axis_index("leaf")
    rounds = 4
    line = 16
    leaves, leaf_size = near_mat.shape[0], near_mat.shape[1]
    scale = 1.0 / leaf_size
    rank = parent.shape[1]
    rhs = vec.shape[0]
    local = rounds * PER_ROUND
    blocks = order.shape[0]
    bits = [(me // (1 << u)) % 2 for u in range(2 * rounds)]

    def partner(g, t):
        step = 1 << (2 * g)
        low = (1 - 2 * bits[2 * g]) * step
        high = (1 - 2 * bits[2 * g + 1]) * (2 * step)
        return me + (t % 2) * low + (t // 2) * high

    def on_line(t):
        return me + sum((1 - 2 * bits[u]) * (1 << u) for u in range(4) if t >> u & 1)

    def on_plane(t):
        return me + sum((1 - 2 * bits[u + 4]) * (1 << (u + 4)) for u in range(4) if t >> u & 1)

    barrier = pltpu.get_barrier_semaphore()
    for t in range(1, line):
        pl.semaphore_signal(barrier, inc=1, device_id=(on_line(t),), device_id_type=MESH)
        pl.semaphore_signal(barrier, inc=1, device_id=(on_plane(t),), device_id_type=MESH)

    def copies(src, dst, sent, received, g):
        return [
            pltpu.make_async_remote_copy(
                src_ref=src,
                dst_ref=dst.at[t - 1],
                send_sem=sent.at[t - 1],
                recv_sem=received.at[t - 1],
                device_id=(partner(g, t),),
                device_id_type=MESH,
            )
            for t in range(1, 4)
        ]

    def line_copies(phase):
        return [
            pltpu.make_async_remote_copy(
                src_ref=line_out,
                dst_ref=line_in.at[phase, t - 1],
                send_sem=line_send.at[t - 1],
                recv_sem=line_recv.at[phase, t - 1],
                device_id=(on_line(t),),
                device_id_type=MESH,
            )
            for t in range(1, line)
        ]

    def plane_copies():
        return [
            pltpu.make_async_remote_copy(
                src_ref=line_out,
                dst_ref=plane_in.at[t - 1],
                send_sem=line_send.at[t - 1],
                recv_sem=plane_recv.at[t - 1],
                device_id=(on_plane(t),),
                device_id_type=MESH,
            )
            for t in range(1, line)
        ]

    tile_lane = lax.broadcasted_iota(jnp.int32, (8, LANES), 1)

    def to_tile(column):
        return jnp.where(tile_lane == 0, column[0:8], jnp.where(tile_lane == 1, column[8:16], 0.0))

    def from_tile(tile):
        return jnp.concatenate([tile[:, 0:1], tile[:, 1:2]], axis=0)

    def tile_copies(phase, n):
        return copies(tile_out.at[n], tile_in.at[phase, n], tile_send.at[n], tile_recv.at[phase, n], n + 2)

    def tile_sum(phase, n):
        return (tile_out[n] + tile_in[phase, n, 0]) + (tile_in[phase, n, 1] + tile_in[phase, n, 2])

    def line_sum(got):
        parts = [line_out[...]] + [got[t] for t in range(line - 1)]
        while len(parts) > 1:
            parts = [a + b for a, b in zip(parts[0::2], parts[1::2])]
        return parts[0]

    def keep(slot, value):
        high, low = split(value)
        t_hi[slot] = high
        t_lo[slot] = low

    def times(stacked, slot):
        return fold3(mm(stacked, t_hi[slot]) + mm(stacked, t_lo[slot]))

    def times_t(stacked, slot):
        return fold3(mm_t(stacked, t_hi[slot]) + mm_t(stacked, t_lo[slot]))

    def choose(first_is_own, index_row, own, other):
        swapped = jnp.where(index_row >= rank, index_row - rank, index_row + rank)
        want = jnp.where(first_is_own, index_row, swapped)
        place = lax.broadcasted_iota(jnp.int32, (rank, rank), 0).astype(F32)
        got = None
        for n, points in enumerate((own, other)):
            hot = jnp.where(place + float(n * rank) == want, 1.0, 0.0).astype(BF16)
            part = fold3(mm(stack3(points), hot))
            got = part if got is None else got + part
        return got

    def place_points(ob, carry):
        row = order[pl.ds(ob, 1), :]
        span = pl.ds(pl.multiple_of(ob * LANES, LANES), LANES)
        pts[:, span] = pick([block_of(coords)], row, 0, blocks)[0]
        place = ob * LANES + lax.broadcasted_iota(jnp.int32, (blocks, LANES), 1)
        hit = lax.broadcasted_iota(jnp.int32, (blocks, LANES), 0) == (row >> 7)
        digits[0:blocks, span] = jnp.where(hit, (place >> 5).astype(F32), 0.0).astype(BF16)
        digits[blocks : 2 * blocks, span] = jnp.where(hit, (place & 31).astype(F32), 0.0).astype(BF16)
        lane_hit = lax.broadcasted_iota(jnp.int32, (LANES, LANES), 0) == (row & (LANES - 1))
        marks[:, span] = jnp.where(lane_hit, 1.0, 0.0).astype(BF16)
        return carry

    lax.fori_loop(0, blocks // 4, lambda group, carry: [place_points(group * 4 + n, carry) for n in range(4)][-1], 0)
    leaf_blocks = blocks // leaves
    per = rank // LANES
    for leaf in range(leaves):
        for ob in range(per):
            row = leaf_skel[leaf : leaf + 1, ob * LANES : (ob + 1) * LANES]
            (got,) = pick([block_of(pts)], row, leaf * leaf_blocks, leaf_blocks)
            skel[leaf, :, ob * LANES : (ob + 1) * LANES] = got
    both = lambda b: skel[b // per, :, (b % per) * LANES : (b % per + 1) * LANES]
    for ob in range(per):
        row = local_skel[0:1, ob * LANES : (ob + 1) * LANES]
        (got,) = pick([both], row, 0, 2 * per)
        parent[:, ob * LANES : (ob + 1) * LANES] = got
    pl.semaphore_wait(barrier, 2 * (line - 1))

    def place_state():
        sources = [block_of(r_in), block_of(p_in)]

        def body(group, carry):
            for n in range(4):
                ob = group * 4 + n
                span = pl.ds(pl.multiple_of(ob * LANES, LANES), LANES)
                got = pick(sources, order[pl.ds(ob, 1), :], 0, blocks)
                r_ref[:, span] = got[0]
                vec[:, span] = got[1]
            return carry

        lax.fori_loop(0, blocks // 4, body, 0)
        found = mm_t(digits[...], marks[...])
        inverse[...] = (found[0:blocks] * 32.0 + found[blocks : 2 * blocks]).astype(jnp.int32)

    def make_near():
        for leaf in range(leaves):
            cols = slice(leaf * leaf_size, (leaf + 1) * leaf_size)
            lefts[leaf] = left_form(pts[:, cols])
            rights[:, cols] = right_form(pts[:, cols])

            def body(j, carry, leaf=leaf, cols=cols):
                span = pl.ds(pl.multiple_of(j * rank, rank), rank)
                near_mat[leaf, span, :] = jnp.exp2(mm(lefts[leaf, span, :], rights[:, cols])).astype(BF16)
                return carry

            lax.fori_loop(0, leaf_size // rank, body, 0)

    def make_basis(leaf):
        left = left_form(skel[leaf])

        def body(group, carry):
            for n in range(4):
                j = group * 4 + n
                inner = pl.ds(pl.multiple_of(j * rank, rank), rank)
                span = pl.ds(pl.multiple_of(leaf * leaf_size + j * rank, rank), rank)
                high, low = split(softmax2(mm(left, rights[:, span]), 0))
                ut_hi[leaf, :, inner] = high
                ut_lo[leaf, :, inner] = low
            return carry

        lax.fori_loop(0, leaf_size // rank // 4, body, 0)

    def make_local():
        skel_left = [left_form(skel[leaf]) for leaf in range(leaves)]
        parent_right = right_form(parent[...])
        for leaf in range(leaves):
            keep(local + leaf, softmax2(mm(skel_left[leaf], parent_right), 1))
        keep(local + 2, jnp.exp2(mm(skel_left[0], right_form(skel[1]))) * scale)

    def make_round(g):
        base = g * PER_ROUND
        low = [points_out[g, 0:16, :]] + [points_in[g, t, 0:16, :] for t in range(3)]
        mids = [middles[g, n] for n in range(2)]
        low_left = [left_form(x) for x in low]
        mid_left = [left_form(x) for x in mids]
        mid_right = [right_form(x) for x in mids]
        for t in range(4):
            keep(base + OWN0 + t, softmax2(mm(low_left[t], mid_right[t // 2]), 1))
        keep(base + SIB, jnp.exp2(mm(low_left[1], right_form(low[0]))) * scale)
        keep(base + COUSIN, jnp.exp2(mm(low_left[3], right_form(low[2]))) * scale)
        keep(base + UNCLE, jnp.exp2(mm(mid_left[1], mid_right[0])) * scale)
        if g + 1 < rounds:
            top_right = right_form(points_out[g + 1, 0:16, :])
            for n in range(2):
                keep(base + UP0 + n, softmax2(mm(mid_left[n], top_right), 1))

    beside = [
        (place_state,),
        (make_near,),
        (lambda: make_basis(0), lambda: make_round(0)),
        (lambda: make_basis(1), lambda: make_round(1), make_local),
    ]
    own = parent[...]
    for g in range(rounds):
        u = 2 * g
        points_out[g, 0:16, :] = own
        points_out[g, 16:24, :] = jnp.broadcast_to(upper[u].astype(F32), (8, rank))
        sends = copies(points_out.at[g], points_in.at[g], send_sem.at[g], recv_sem.at[0, g], g)
        for c in sends:
            c.start()
        for work in beside[g]:
            work()
        for c in sends:
            c.wait()
        low = [own] + [points_in[g, t, 0:16, :] for t in range(3)]
        lists = [points_out[g, 16:17, :], points_in[g, 1, 16:17, :]]
        mids = [choose(bits[u] == 0, lists[n], low[2 * n], low[2 * n + 1]) for n in range(2)]
        for n in range(2):
            middles[g, n] = mids[n]
        if g + 1 < rounds:
            own = choose(bits[u + 1] == 0, upper[u + 1].astype(F32), mids[0], mids[1])

    p_ref[...] = jnp.zeros_like(p_ref)
    q_ref[...] = jnp.zeros_like(q_ref)
    gain[...] = jnp.zeros_like(gain)
    state[0] = jnp.ones(state.shape[1:], F32)
    state[1] = jnp.zeros(state.shape[1:], F32)
    state[2] = jnp.zeros(state.shape[1:], F32)
    lane = lax.broadcasted_iota(jnp.int32, (rhs, LANES), 1)

    def near_product(leaf):
        def body(j, carry):
            inner = pl.ds(pl.multiple_of(j * rank, rank), rank)
            span = pl.ds(pl.multiple_of(leaf * leaf_size + j * rank, rank), rank)
            wide = fold3(mm(vsplit[:, leaf * leaf_size : (leaf + 1) * leaf_size], near_mat[leaf, :, inner]))
            image[:, span] = 0.5 * vec[:, span] + wide * scale
            return carry

        lax.fori_loop(0, leaf_size // rank, body, 0)

    def iteration(k, carry):
        vsplit[...] = stack3(vec[...])
        leaf_coef = []
        for leaf in range(leaves):
            part = vsplit[:, leaf * leaf_size : (leaf + 1) * leaf_size]
            leaf_coef.append(fold3(mm_t(part, ut_hi[leaf]) + mm_t(part, ut_lo[leaf])))
        wide = [stack3(x) for x in leaf_coef]
        coef = times(wide[0], local) + times(wide[1], local + 1)
        last = None
        for g in range(rounds):
            base = g * PER_ROUND
            coef_out[g] = coef
            sends = copies(coef_out.at[g], coef_in.at[k, g], send_sem.at[g], recv_sem.at[1 + k, g], g)
            for c in sends:
                c.start()
            if g == 0:
                leaf_cp = [times_t(wide[1], local + 2), times(wide[0], local + 2)]
                sums = jnp.where(lane == 0, row_dot(r_ref[...], r_ref[...]), 0.0)
                sums = jnp.where(lane == 1, row_dot(vec[...], q_ref[...]), sums)
                sums = jnp.where(lane == 3, row_dot(r_ref[...], vec[...]), sums)
                sums = jnp.where(lane == 4, row_dot(vec[...], vec[...]), sums)
                sums = jnp.where(lane == 2, 2.0 * row_dot(leaf_coef[0], leaf_cp[0]), sums)
            else:
                sums = last()
            sums_out[g] = sums
            sum_sends = copies(sums_out.at[g], sums_in.at[k, g], sums_send.at[g], sums_recv.at[k, g], g)
            for c in sum_sends:
                c.start()
            if g < leaves:
                near_product(g)
            if g == 1:
                line_out[...] = to_tile(row_dot(vec[...], image[...]))
                side = line_copies(k)
            else:
                if g > 1:
                    for c in side:
                        c.wait()
                    tile_out[g - 2] = line_sum(line_in.at[k]) if g == 2 else tile_sum(k, 0)
                    side = tile_copies(k, g - 2)
            if g > 0:
                for c in side:
                    c.start()
            if g in (1, 2):
                pl.when(k == 0)(lambda g=g: make_round(g + 1))
            for c in sends:
                c.wait()
            got = [coef] + [coef_in[k, g, t] for t in range(3)]
            wide = [stack3(x) for x in got]
            mid0 = times(wide[0], base + OWN0) + times(wide[1], base + OWN1)
            mid1 = times(wide[2], base + OWN2) + times(wide[3], base + OWN3)
            mid1_wide = stack3(mid1)
            if g + 1 < rounds:
                coef = times(stack3(mid0), base + UP0) + times(mid1_wide, base + UP1)

            def last(g=g, base=base, got=got, wide=wide, mid0=mid0, mid1_wide=mid1_wide, sums=sums, sent=sum_sends):
                low_cp = times(wide[1], base + SIB)
                mid_cp = times(mid1_wide, base + UNCLE)
                cps[2 * g] = low_cp
                cps[2 * g + 1] = mid_cp
                quad = row_dot(got[0], low_cp) + row_dot(got[2], times(wide[3], base + COUSIN)) + row_dot(mid0, mid_cp)
                for c in sent:
                    c.wait()
                far = [sums_in[k, g, t] for t in range(3)]
                return (sums + far[0]) + (far[1] + far[2]) + jnp.where(lane == 2, 2.0 * quad, 0.0)

        sums = last()
        down = cps[2 * rounds - 1]
        for u in range(2 * rounds - 2, -1, -1):
            down = cps[u] + times_t(stack3(down), (u // 2) * PER_ROUND + (UP0 if u % 2 else OWN0))
        down_wide = stack3(down)
        for leaf in range(leaves):
            cols = slice(leaf * leaf_size, (leaf + 1) * leaf_size)
            part = stack3(leaf_cp[leaf] + times_t(down_wide, local + leaf))
            image[:, cols] += fold3(mm(part, ut_hi[leaf]) + mm(part, ut_lo[leaf]))
        for c in side:
            c.wait()
        near = from_tile(tile_sum(k, 1))
        fresh = sums[:, 0:1]
        cross = sums[:, 1:2]
        beta = fresh / state[0, :, 0:1] - state[2, :, 0:1]
        guess = jnp.where(k == 0, 1.0 + (fresh - 2.0 * sums[:, 3:4]) / sums[:, 4:5], 0.0)
        state[2] = jnp.broadcast_to(guess, (rhs, LANES))
        curve = (sums[:, 2:3] + near) + 2.0 * beta * cross + beta * beta * state[1, :, 0:1]
        alpha = fresh / curve
        state[0] = jnp.broadcast_to(fresh, (rhs, LANES))
        state[1] = jnp.broadcast_to(curve, (rhs, LANES))
        p_new = vec[...] + beta * p_ref[...]
        q_new = image[...] + beta * q_ref[...]
        p_ref[...] = p_new
        q_ref[...] = q_new
        gain[...] += alpha * p_new
        r_new = r_ref[...] - alpha * q_new
        r_ref[...] = r_new
        vec[...] = r_new + guess * p_new
        return carry

    lax.fori_loop(0, ITERS, iteration, 0)

    sources = [block_of(gain), block_of(r_ref), block_of(p_ref)]

    def restore(group, carry):
        for n in range(4):
            ob = group * 4 + n
            span = pl.ds(pl.multiple_of(ob * LANES, LANES), LANES)
            got = pick(sources, inverse[pl.ds(ob, 1), :], 0, blocks)
            x_out[:, span] = x_in[:, span] + got[0]
            r_out[:, span] = got[1]
            p_out[:, span] = got[2]
        return carry

    line_out[...] = to_tile(row_dot(r_ref[...], r_ref[...]))
    sends = line_copies(ITERS)
    for c in sends:
        c.start()
    lax.fori_loop(0, blocks // 8, restore, 0)
    for c in sends:
        c.wait()
    line_out[...] = line_sum(line_in.at[ITERS])
    sends = plane_copies()
    for c in sends:
        c.start()
    lax.fori_loop(blocks // 8, blocks // 4, restore, 0)
    for c in sends:
        c.wait()
    tile = line_sum(plane_in)
    p_out[...] = r_out[...] + from_tile(tile) / state[0, :, 0:1] * p_out[...]


def per_device(coords, solution, residual, direction, order, leaf_skel, local_skel, upper_skel):
    dims, count = coords.shape
    rhs = solution.shape[0]
    leaves, rank = leaf_skel.shape
    leaf_size = count // leaves
    blocks = count // LANES
    flat = jax.ShapeDtypeStruct((rhs, count), F32)
    slots = 4 * PER_ROUND + 3
    return pl.pallas_call(
        solve,
        out_shape=(flat, flat, flat),
        in_specs=[VMEM] * 8,
        out_specs=(VMEM,) * 3,
        scratch_shapes=[
            pltpu.VMEM((leaves, leaf_size, leaf_size), BF16),
            pltpu.VMEM((leaves, leaf_size, LANES), BF16),
            pltpu.VMEM((LANES, count), BF16),
            pltpu.VMEM((leaves, rank, leaf_size), BF16),
            pltpu.VMEM((leaves, rank, leaf_size), BF16),
            pltpu.VMEM((slots, rank, rank), BF16),
            pltpu.VMEM((slots, rank, rank), BF16),
            pltpu.VMEM((dims, count), F32),
            pltpu.VMEM((rhs, count), F32),
            pltpu.VMEM((3 * rhs, count), BF16),
            pltpu.VMEM((rhs, count), F32),
            pltpu.VMEM((rhs, count), F32),
            pltpu.VMEM((rhs, count), F32),
            pltpu.VMEM((rhs, count), F32),
            pltpu.VMEM((rhs, count), F32),
            pltpu.VMEM((2 * blocks, count), BF16),
            pltpu.VMEM((LANES, count), BF16),
            pltpu.VMEM((blocks, LANES), jnp.int32),
            pltpu.VMEM((leaves, dims, rank), F32),
            pltpu.VMEM((dims, rank), F32),
            pltpu.VMEM((3, rhs, LANES), F32),
            pltpu.VMEM((8, rhs, rank), F32),
            pltpu.VMEM((4, dims + 8, rank), F32),
            pltpu.VMEM((4, 3, dims + 8, rank), F32),
            pltpu.VMEM((4, rhs, rank), F32),
            pltpu.VMEM((ITERS, 4, 3, rhs, rank), F32),
            pltpu.VMEM((4, rhs, LANES), F32),
            pltpu.VMEM((ITERS, 4, 3, rhs, LANES), F32),
            pltpu.VMEM((4, 2, dims, rank), F32),
            pltpu.VMEM((8, LANES), F32),
            pltpu.VMEM((ITERS + 1, 15, 8, LANES), F32),
            pltpu.VMEM((15, 8, LANES), F32),
            pltpu.VMEM((2, 8, LANES), F32),
            pltpu.VMEM((ITERS, 2, 3, 8, LANES), F32),
            pltpu.SemaphoreType.DMA((4, 3)),
            pltpu.SemaphoreType.DMA((ITERS + 1, 4, 3)),
            pltpu.SemaphoreType.DMA((4, 3)),
            pltpu.SemaphoreType.DMA((ITERS, 4, 3)),
            pltpu.SemaphoreType.DMA((15,)),
            pltpu.SemaphoreType.DMA((ITERS + 1, 15)),
            pltpu.SemaphoreType.DMA((15,)),
            pltpu.SemaphoreType.DMA((2, 3)),
            pltpu.SemaphoreType.DMA((ITERS, 2, 3)),
        ],
        compiler_params=pltpu.CompilerParams(
            vmem_limit_bytes=56 * 1024 * 1024, collective_id=0, has_side_effects=True
        ),
    )(
        coords,
        solution,
        residual,
        direction,
        order.reshape(blocks, LANES),
        leaf_skel,
        local_skel,
        upper_skel,
    )


def solution(mesh):
    in_specs = (
        P(None, "leaf"),
        P(None, "leaf"),
        P(None, "leaf"),
        P(None, "leaf"),
        P("leaf"),
        P("leaf", None),
        P("leaf", None),
        P(None, "leaf", None),
    )
    out_specs = (P(None, "leaf"), P(None, "leaf"), P(None, "leaf"))
    return jax.shard_map(
        per_device, mesh=mesh, in_specs=in_specs, out_specs=out_specs, check_vma=False
    )
```

```python
import math

import jax
import jax.numpy as jnp
from jax import lax
from jax.experimental import pallas as pl
from jax.experimental.pallas import tpu as pltpu
from jax.sharding import PartitionSpec as P

ITERS = 4
MESH = pl.DeviceIdType.MESH
LANES = 128
LOG2E = math.log2(math.e)
F32 = jnp.float32
BF16 = jnp.bfloat16
VMEM = pl.BlockSpec(memory_space=pltpu.VMEM)

OWN0, OWN1, OWN2, OWN3, UP0, UP1, SIB, COUSIN, UNCLE = range(9)
PER_ROUND = 9


def pick(sources, index_row, first_block, block_count):
    low = index_row & (LANES - 1)
    high = index_row >> 7
    outs = [None] * len(sources)
    for block in range(block_count):
        hit = None
        for n, source in enumerate(sources):
            held = source(first_block + block)
            rows = held.shape[0]
            place = jnp.broadcast_to(low, (rows, LANES))
            got = jnp.take_along_axis(held, place, axis=1, mode="promise_in_bounds")
            if outs[n] is None:
                outs[n] = got
            else:
                hit = jnp.broadcast_to(high, (rows, LANES)) == block
                outs[n] = jnp.where(hit, got, outs[n])
    return outs


def block_of(ref):
    return lambda b: ref[:, b * LANES : (b + 1) * LANES]


def split(value):
    high = value.astype(BF16)
    return high, (value - high.astype(F32)).astype(BF16)


def split3(value):
    high = value.astype(BF16)
    rest = value - high.astype(F32)
    mid = rest.astype(BF16)
    return high, mid, (rest - mid.astype(F32)).astype(BF16)


def mm(a, b):
    return jnp.dot(a, b, preferred_element_type=F32)


def mm_t(a, b):
    return lax.dot_general(a, b, (((1,), (1,)), ((), ())), preferred_element_type=F32)


def stack3(value):
    return jnp.concatenate(split3(value), axis=0)


def fold3(wide):
    rows = wide.shape[0] // 3
    return wide[:rows] + (wide[rows : 2 * rows] + wide[2 * rows :])


def norm_rows(norms, first):
    high, mid, low = (part.astype(F32) for part in split3(norms))
    shape = (16, norms.shape[1])
    row = lax.broadcasted_iota(jnp.int32, shape, 0)
    one = jnp.where((row >= 3 - first) & (row < 6 - first), 1.0, 0.0)
    tile = jnp.where(row == first, high, one)
    tile = jnp.where(row == first + 1, mid, tile)
    return jnp.where(row == first + 2, low, tile)


def left_form(points):
    high, mid, low = (part.astype(F32) for part in split3(points))
    norms = jnp.sum(points * points, axis=0, keepdims=True) * (-LOG2E / 32.0)
    extra = norm_rows(norms, 0)
    full = jnp.concatenate([high, high, mid, mid, high, low, extra, jnp.zeros_like(extra)], axis=0)
    return jnp.transpose(full, (1, 0)).astype(BF16)


def right_form(points):
    high, mid, low = split3(points * (LOG2E / 16.0))
    norms = jnp.sum(points * points, axis=0, keepdims=True) * (-LOG2E / 32.0)
    extra = norm_rows(norms, 3).astype(BF16)
    return jnp.concatenate([high, mid, high, mid, low, high, extra, jnp.zeros_like(extra)], axis=0)


def softmax2(scores, axis):
    weights = jnp.exp2(scores - jnp.max(scores, axis=axis, keepdims=True))
    return weights * (1.0 / jnp.sum(weights, axis=axis, keepdims=True))


def row_dot(a, b):
    return jnp.sum(a * b, axis=1, keepdims=True)


def solve(coords, x_in, r_in, p_in, order, leaf_skel, local_skel, upper, x_out, r_out, p_out,
          near_mat, lefts, rights, ut_hi, ut_lo, t_hi, t_lo, pts, vec, vsplit, image, q_ref, r_ref, p_ref, gain,
          digits, marks, inverse, skel, parent, state, cps,
          points_out, points_in, coef_out, coef_in, sums_out, sums_in, middles, coefs, line_out, line_in, plane_out, plane_in,
          send_sem, recv_sem, sums_send, sums_recv, line_send, line_recv, plane_send, plane_recv):
    me = lax.axis_index("leaf")
    rounds = 4
    line = 16
    leaves, leaf_size = near_mat.shape[0], near_mat.shape[1]
    scale = 1.0 / leaf_size
    rank = parent.shape[1]
    rhs = vec.shape[0]
    local = rounds * PER_ROUND
    blocks = order.shape[0]
    bits = [(me // (1 << u)) % 2 for u in range(2 * rounds)]

    def partner(g, t):
        step = 1 << (2 * g)
        low = (1 - 2 * bits[2 * g]) * step
        high = (1 - 2 * bits[2 * g + 1]) * (2 * step)
        return me + (t % 2) * low + (t // 2) * high

    def on_line(t):
        return me + sum((1 - 2 * bits[u]) * (1 << u) for u in range(4) if t >> u & 1)

    def on_plane(t):
        return me + sum((1 - 2 * bits[u + 4]) * (1 << (u + 4)) for u in range(4) if t >> u & 1)

    barrier = pltpu.get_barrier_semaphore()
    for t in range(1, line):
        pl.semaphore_signal(barrier, inc=1, device_id=(on_line(t),), device_id_type=MESH)
        pl.semaphore_signal(barrier, inc=1, device_id=(on_plane(t),), device_id_type=MESH)

    def copies(src, dst, sent, received, g):
        return [
            pltpu.make_async_remote_copy(
                src_ref=src,
                dst_ref=dst.at[t - 1],
                send_sem=sent.at[t - 1],
                recv_sem=received.at[t - 1],
                device_id=(partner(g, t),),
                device_id_type=MESH,
            )
            for t in range(1, 4)
        ]

    def line_copies(phase):
        return [
            pltpu.make_async_remote_copy(
                src_ref=line_out,
                dst_ref=line_in.at[phase, t - 1],
                send_sem=line_send.at[t - 1],
                recv_sem=line_recv.at[phase, t - 1],
                device_id=(on_line(t),),
                device_id_type=MESH,
            )
            for t in range(1, line)
        ]

    def plane_copies(phase):
        return [
            pltpu.make_async_remote_copy(
                src_ref=plane_out,
                dst_ref=plane_in.at[phase, t - 1],
                send_sem=plane_send.at[t - 1],
                recv_sem=plane_recv.at[phase, t - 1],
                device_id=(on_plane(t),),
                device_id_type=MESH,
            )
            for t in range(1, line)
        ]

    tile_lane = lax.broadcasted_iota(jnp.int32, (8, LANES), 1)

    def to_tile(*columns):
        tile = jnp.zeros((8, LANES), F32)
        for n, column in enumerate(columns):
            tile = jnp.where(tile_lane == 2 * n, column[0:8], tile)
            tile = jnp.where(tile_lane == 2 * n + 1, column[8:16], tile)
        return tile

    def from_tile(tile, n=0):
        return jnp.concatenate([tile[:, 2 * n : 2 * n + 1], tile[:, 2 * n + 1 : 2 * n + 2]], axis=0)

    def line_sum(own, got):
        parts = [own[...]] + [got[t] for t in range(line - 1)]
        while len(parts) > 1:
            parts = [a + b for a, b in zip(parts[0::2], parts[1::2])]
        return parts[0]

    def keep(slot, value):
        high, low = split(value)
        t_hi[slot] = high
        t_lo[slot] = low

    def times(stacked, slot):
        return fold3(mm(stacked, t_hi[slot]) + mm(stacked, t_lo[slot]))

    def times_t(stacked, slot):
        return fold3(mm_t(stacked, t_hi[slot]) + mm_t(stacked, t_lo[slot]))

    def choose(first_is_own, index_row, own, other):
        swapped = jnp.where(index_row >= rank, index_row - rank, index_row + rank)
        want = jnp.where(first_is_own, index_row, swapped)
        place = lax.broadcasted_iota(jnp.int32, (rank, rank), 0).astype(F32)
        got = None
        for n, points in enumerate((own, other)):
            hot = jnp.where(place + float(n * rank) == want, 1.0, 0.0).astype(BF16)
            part = fold3(mm(stack3(points), hot))
            got = part if got is None else got + part
        return got

    def place_points(ob, carry):
        row = order[pl.ds(ob, 1), :]
        span = pl.ds(pl.multiple_of(ob * LANES, LANES), LANES)
        pts[:, span] = pick([block_of(coords)], row, 0, blocks)[0]
        place = ob * LANES + lax.broadcasted_iota(jnp.int32, (blocks, LANES), 1)
        hit = lax.broadcasted_iota(jnp.int32, (blocks, LANES), 0) == (row >> 7)
        digits[0:blocks, span] = jnp.where(hit, (place >> 5).astype(F32), 0.0).astype(BF16)
        digits[blocks : 2 * blocks, span] = jnp.where(hit, (place & 31).astype(F32), 0.0).astype(BF16)
        lane_hit = lax.broadcasted_iota(jnp.int32, (LANES, LANES), 0) == (row & (LANES - 1))
        marks[:, span] = jnp.where(lane_hit, 1.0, 0.0).astype(BF16)
        return carry

    lax.fori_loop(0, blocks // 4, lambda group, carry: [place_points(group * 4 + n, carry) for n in range(4)][-1], 0)
    leaf_blocks = blocks // leaves
    per = rank // LANES
    for leaf in range(leaves):
        for ob in range(per):
            row = leaf_skel[leaf : leaf + 1, ob * LANES : (ob + 1) * LANES]
            (got,) = pick([block_of(pts)], row, leaf * leaf_blocks, leaf_blocks)
            skel[leaf, :, ob * LANES : (ob + 1) * LANES] = got
    both = lambda b: skel[b // per, :, (b % per) * LANES : (b % per + 1) * LANES]
    for ob in range(per):
        row = local_skel[0:1, ob * LANES : (ob + 1) * LANES]
        (got,) = pick([both], row, 0, 2 * per)
        parent[:, ob * LANES : (ob + 1) * LANES] = got
    pl.semaphore_wait(barrier, 2 * (line - 1))

    def place_state(source, target):
        def body(group, carry):
            for n in range(4):
                ob = group * 4 + n
                span = pl.ds(pl.multiple_of(ob * LANES, LANES), LANES)
                target[:, span] = pick([block_of(source)], order[pl.ds(ob, 1), :], 0, blocks)[0]
            return carry

        lax.fori_loop(0, blocks // 4, body, 0)

    def invert():
        found = mm_t(digits[...], marks[...])
        inverse[...] = (found[0:blocks] * 32.0 + found[blocks : 2 * blocks]).astype(jnp.int32)

    def make_near():
        for leaf in range(leaves):
            cols = slice(leaf * leaf_size, (leaf + 1) * leaf_size)
            lefts[leaf] = left_form(pts[:, cols])
            rights[:, cols] = right_form(pts[:, cols])

            def body(j, carry, leaf=leaf, cols=cols):
                span = pl.ds(pl.multiple_of(j * rank, rank), rank)
                near_mat[leaf, span, :] = jnp.exp2(mm(lefts[leaf, span, :], rights[:, cols])).astype(BF16)
                return carry

            lax.fori_loop(0, leaf_size // rank, body, 0)

    def make_basis(leaf):
        left = left_form(skel[leaf])

        def body(group, carry):
            for n in range(4):
                j = group * 4 + n
                inner = pl.ds(pl.multiple_of(j * rank, rank), rank)
                span = pl.ds(pl.multiple_of(leaf * leaf_size + j * rank, rank), rank)
                high, low = split(softmax2(mm(left, rights[:, span]), 0))
                ut_hi[leaf, :, inner] = high
                ut_lo[leaf, :, inner] = low
            return carry

        lax.fori_loop(0, leaf_size // rank // 4, body, 0)

    def make_local():
        skel_left = [left_form(skel[leaf]) for leaf in range(leaves)]
        parent_right = right_form(parent[...])
        for leaf in range(leaves):
            keep(local + leaf, softmax2(mm(skel_left[leaf], parent_right), 1))
        keep(local + 2, jnp.exp2(mm(skel_left[0], right_form(skel[1]))) * scale)

    def make_gram():
        for leaf in range(leaves):
            high, low = ut_hi[leaf], ut_lo[leaf]
            cross = mm_t(high, low)
            keep(local + 3 + leaf, mm_t(high, high) + (cross + jnp.transpose(cross, (1, 0))))

    def make_round(g):
        base = g * PER_ROUND
        low = [points_out[g, 0:16, :]] + [points_in[g, t, 0:16, :] for t in range(3)]
        mids = [middles[g, n] for n in range(2)]
        low_left = [left_form(x) for x in low]
        mid_left = [left_form(x) for x in mids]
        mid_right = [right_form(x) for x in mids]
        for t in range(4):
            keep(base + OWN0 + t, softmax2(mm(low_left[t], mid_right[t // 2]), 1))
        keep(base + SIB, jnp.exp2(mm(low_left[1], right_form(low[0]))) * scale)
        keep(base + COUSIN, jnp.exp2(mm(low_left[3], right_form(low[2]))) * scale)
        keep(base + UNCLE, jnp.exp2(mm(mid_left[1], mid_right[0])) * scale)
        if g + 1 < rounds:
            top_right = right_form(points_out[g + 1, 0:16, :])
            for n in range(2):
                keep(base + UP0 + n, softmax2(mm(mid_left[n], top_right), 1))

    beside = [
        (lambda: place_state(p_in, vec),),
        (make_near,),
        (lambda: make_basis(0), lambda: make_round(0)),
        (lambda: make_basis(1), lambda: make_round(1), make_local),
    ]
    own = parent[...]
    for g in range(rounds):
        u = 2 * g
        points_out[g, 0:16, :] = own
        points_out[g, 16:24, :] = jnp.broadcast_to(upper[u].astype(F32), (8, rank))
        sends = copies(points_out.at[g], points_in.at[g], send_sem.at[g], recv_sem.at[0, g], g)
        for c in sends:
            c.start()
        for work in beside[g]:
            work()
        for c in sends:
            c.wait()
        low = [own] + [points_in[g, t, 0:16, :] for t in range(3)]
        lists = [points_out[g, 16:17, :], points_in[g, 1, 16:17, :]]
        mids = [choose(bits[u] == 0, lists[n], low[2 * n], low[2 * n + 1]) for n in range(2)]
        for n in range(2):
            middles[g, n] = mids[n]
        if g + 1 < rounds:
            own = choose(bits[u + 1] == 0, upper[u + 1].astype(F32), mids[0], mids[1])

    p_ref[...] = jnp.zeros_like(p_ref)
    q_ref[...] = jnp.zeros_like(q_ref)
    gain[...] = jnp.zeros_like(gain)
    state[0] = jnp.ones(state.shape[1:], F32)
    for n in range(1, state.shape[0]):
        state[n] = jnp.zeros(state.shape[1:], F32)
    lane = lax.broadcasted_iota(jnp.int32, (rhs, LANES), 1)
    OF_V, OF_R, OF_P, OF_Q, OF_NEAR, DOWN = range(6)

    def columns(leaf):
        return slice(leaf * leaf_size, (leaf + 1) * leaf_size)

    def leaf_up(ref, leaf):
        part = stack3(ref[:, columns(leaf)])
        return fold3(mm_t(part, ut_hi[leaf]) + mm_t(part, ut_lo[leaf]))

    def near_product(leaf, first, last):
        def body(j, carry):
            inner = pl.ds(pl.multiple_of(j * rank, rank), rank)
            span = pl.ds(pl.multiple_of(leaf * leaf_size + j * rank, rank), rank)
            wide = fold3(mm(vsplit[:, columns(leaf)], near_mat[leaf, :, inner]))
            image[:, span] = 0.5 * vec[:, span] + wide * scale
            return carry

        lax.fori_loop(first, last, body, 0)

    def finish():
        alpha, beta, guess = (state[n, :, 0:1] for n in (3, 4, 2))
        for leaf in range(leaves):
            cols = columns(leaf)
            part = stack3(coefs[DOWN, leaf])
            full = image[:, cols] + fold3(mm(part, ut_hi[leaf]) + mm(part, ut_lo[leaf]))
            p_new = vec[:, cols] + beta * p_ref[:, cols]
            q_new = full + beta * q_ref[:, cols]
            p_ref[:, cols] = p_new
            q_ref[:, cols] = q_new
            gain[:, cols] += alpha * p_new
            r_new = r_ref[:, cols] - alpha * q_new
            r_ref[:, cols] = r_new
            vec[:, cols] = r_new + guess * p_new

    for leaf in range(leaves):
        coefs[OF_V, leaf] = leaf_up(vec, leaf)
        coefs[OF_P, leaf] = jnp.zeros(coefs.shape[2:], F32)
        coefs[OF_Q, leaf] = jnp.zeros(coefs.shape[2:], F32)
    chunks = leaf_size // rank

    def iteration(k, carry):
        leaf_coef = [coefs[OF_V, leaf] for leaf in range(leaves)]
        wide = [stack3(x) for x in leaf_coef]
        coef = times(wide[0], local) + times(wide[1], local + 1)
        last = None
        for g in range(rounds):
            base = g * PER_ROUND
            coef_out[g] = coef
            sends = copies(coef_out.at[g], coef_in.at[k, g], send_sem.at[g], recv_sem.at[1 + k, g], g)
            for c in sends:
                c.start()
            if g == 0:
                leaf_cp = [times_t(wide[1], local + 2), times(wide[0], local + 2)]
                sums = jnp.where(lane == 2, 2.0 * row_dot(leaf_coef[0], leaf_cp[0]), 0.0)
            else:
                sums = last()
            sums_out[g] = sums
            sum_sends = copies(sums_out.at[g], sums_in.at[k, g], sums_send.at[g], sums_recv.at[k, g], g)
            for c in sum_sends:
                c.start()
            if g == 0:
                pl.when(k > 0)(finish)
                pl.when(k == 0)(lambda: place_state(r_in, r_ref))
                vsplit[...] = stack3(vec[...])
                near_product(0, 0, chunks // 4)
            if g == 1:
                near_product(0, chunks // 4, chunks)
                near_product(1, 0, chunks)
                line_out[...] = to_tile(
                    row_dot(vec[...], image[...]),
                    row_dot(r_ref[...], r_ref[...]),
                    row_dot(vec[...], q_ref[...]),
                    row_dot(r_ref[...], vec[...]),
                    row_dot(vec[...], vec[...]),
                )
                side = line_copies(k)
                for c in side:
                    c.start()
            if g == 2:
                for leaf in range(leaves):
                    coefs[OF_NEAR, leaf] = leaf_up(image, leaf)
            if g == 3:
                for c in side:
                    c.wait()
                plane_out[...] = line_sum(line_out, line_in.at[k])
                side = plane_copies(k)
                for c in side:
                    c.start()
            if g > 0:

                @pl.when(k == 0)
                def _(g=g):
                    if g < 3:
                        make_round(g + 1)
                    else:
                        make_gram()
                        invert()
                        for leaf in range(leaves):
                            coefs[OF_R, leaf] = leaf_up(r_ref, leaf)

            for c in sends:
                c.wait()
            got = [coef] + [coef_in[k, g, t] for t in range(3)]
            wide = [stack3(x) for x in got]
            mid0 = times(wide[0], base + OWN0) + times(wide[1], base + OWN1)
            mid1 = times(wide[2], base + OWN2) + times(wide[3], base + OWN3)
            mid1_wide = stack3(mid1)
            if g + 1 < rounds:
                coef = times(stack3(mid0), base + UP0) + times(mid1_wide, base + UP1)

            def last(g=g, base=base, got=got, wide=wide, mid0=mid0, mid1_wide=mid1_wide, sums=sums, sent=sum_sends):
                low_cp = times(wide[1], base + SIB)
                mid_cp = times(mid1_wide, base + UNCLE)
                cps[2 * g] = low_cp
                cps[2 * g + 1] = mid_cp
                quad = row_dot(got[0], low_cp) + row_dot(got[2], times(wide[3], base + COUSIN)) + row_dot(mid0, mid_cp)
                for c in sent:
                    c.wait()
                far = [sums_in[k, g, t] for t in range(3)]
                return (sums + far[0]) + (far[1] + far[2]) + jnp.where(lane == 2, 2.0 * quad, 0.0)

        sums = last()
        down = cps[2 * rounds - 1]
        for u in range(2 * rounds - 2, -1, -1):
            down = cps[u] + times_t(stack3(down), (u // 2) * PER_ROUND + (UP0 if u % 2 else OWN0))
        down_wide = stack3(down)
        image_coef = []
        for leaf in range(leaves):
            leaf_down = leaf_cp[leaf] + times_t(down_wide, local + leaf)
            coefs[DOWN, leaf] = leaf_down
            image_coef.append(coefs[OF_NEAR, leaf] + times(stack3(leaf_down), local + 3 + leaf))
        for c in side:
            c.wait()
        tile = line_sum(plane_out, plane_in.at[k])
        near, fresh, cross, with_v, of_v = (from_tile(tile, n) for n in range(5))
        beta = fresh / state[0, :, 0:1] - state[2, :, 0:1]
        guess = jnp.where(k == 0, 1.0 + (fresh - 2.0 * with_v) / of_v, 0.0)
        curve = (sums[:, 2:3] + near) + 2.0 * beta * cross + beta * beta * state[1, :, 0:1]
        alpha = fresh / curve
        for n, column in enumerate((fresh, curve, guess, alpha, beta)):
            state[n] = jnp.broadcast_to(column, (rhs, LANES))
        for leaf in range(leaves):
            p_coef = coefs[OF_V, leaf] + beta * coefs[OF_P, leaf]
            q_coef = image_coef[leaf] + beta * coefs[OF_Q, leaf]
            r_coef = coefs[OF_R, leaf] - alpha * q_coef
            coefs[OF_P, leaf] = p_coef
            coefs[OF_Q, leaf] = q_coef
            coefs[OF_R, leaf] = r_coef
            coefs[OF_V, leaf] = r_coef + guess * p_coef
        return carry

    lax.fori_loop(0, ITERS, iteration, 0)
    finish()

    sources = [block_of(gain), block_of(r_ref), block_of(p_ref)]

    def restore(group, carry):
        for n in range(4):
            ob = group * 4 + n
            span = pl.ds(pl.multiple_of(ob * LANES, LANES), LANES)
            got = pick(sources, inverse[pl.ds(ob, 1), :], 0, blocks)
            x_out[:, span] = x_in[:, span] + got[0]
            r_out[:, span] = got[1]
            p_out[:, span] = got[2]
        return carry

    line_out[...] = to_tile(row_dot(r_ref[...], r_ref[...]))
    sends = line_copies(ITERS)
    for c in sends:
        c.start()
    lax.fori_loop(0, blocks // 8, restore, 0)
    for c in sends:
        c.wait()
    plane_out[...] = line_sum(line_out, line_in.at[ITERS])
    sends = plane_copies(ITERS)
    for c in sends:
        c.start()
    lax.fori_loop(blocks // 8, blocks // 4, restore, 0)
    for c in sends:
        c.wait()
    tile = line_sum(plane_out, plane_in.at[ITERS])
    p_out[...] = r_out[...] + from_tile(tile) / state[0, :, 0:1] * p_out[...]


def per_device(coords, solution, residual, direction, order, leaf_skel, local_skel, upper_skel):
    dims, count = coords.shape
    rhs = solution.shape[0]
    leaves, rank = leaf_skel.shape
    leaf_size = count // leaves
    blocks = count // LANES
    flat = jax.ShapeDtypeStruct((rhs, count), F32)
    slots = 4 * PER_ROUND + 5
    return pl.pallas_call(
        solve,
        out_shape=(flat, flat, flat),
        in_specs=[VMEM] * 8,
        out_specs=(VMEM,) * 3,
        scratch_shapes=[
            pltpu.VMEM((leaves, leaf_size, leaf_size), BF16),
            pltpu.VMEM((leaves, leaf_size, LANES), BF16),
            pltpu.VMEM((LANES, count), BF16),
            pltpu.VMEM((leaves, rank, leaf_size), BF16),
            pltpu.VMEM((leaves, rank, leaf_size), BF16),
            pltpu.VMEM((slots, rank, rank), BF16),
            pltpu.VMEM((slots, rank, rank), BF16),
            pltpu.VMEM((dims, count), F32),
            pltpu.VMEM((rhs, count), F32),
            pltpu.VMEM((3 * rhs, count), BF16),
            pltpu.VMEM((rhs, count), F32),
            pltpu.VMEM((rhs, count), F32),
            pltpu.VMEM((rhs, count), F32),
            pltpu.VMEM((rhs, count), F32),
            pltpu.VMEM((rhs, count), F32),
            pltpu.VMEM((2 * blocks, count), BF16),
            pltpu.VMEM((LANES, count), BF16),
            pltpu.VMEM((blocks, LANES), jnp.int32),
            pltpu.VMEM((leaves, dims, rank), F32),
            pltpu.VMEM((dims, rank), F32),
            pltpu.VMEM((5, rhs, LANES), F32),
            pltpu.VMEM((8, rhs, rank), F32),
            pltpu.VMEM((4, dims + 8, rank), F32),
            pltpu.VMEM((4, 3, dims + 8, rank), F32),
            pltpu.VMEM((4, rhs, rank), F32),
            pltpu.VMEM((ITERS, 4, 3, rhs, rank), F32),
            pltpu.VMEM((4, rhs, LANES), F32),
            pltpu.VMEM((ITERS, 4, 3, rhs, LANES), F32),
            pltpu.VMEM((4, 2, dims, rank), F32),
            pltpu.VMEM((6, leaves, rhs, rank), F32),
            pltpu.VMEM((8, LANES), F32),
            pltpu.VMEM((ITERS + 1, 15, 8, LANES), F32),
            pltpu.VMEM((8, LANES), F32),
            pltpu.VMEM((ITERS + 1, 15, 8, LANES), F32),
            pltpu.SemaphoreType.DMA((4, 3)),
            pltpu.SemaphoreType.DMA((ITERS + 1, 4, 3)),
            pltpu.SemaphoreType.DMA((4, 3)),
            pltpu.SemaphoreType.DMA((ITERS, 4, 3)),
            pltpu.SemaphoreType.DMA((15,)),
            pltpu.SemaphoreType.DMA((ITERS + 1, 15)),
            pltpu.SemaphoreType.DMA((15,)),
            pltpu.SemaphoreType.DMA((ITERS + 1, 15)),
        ],
        compiler_params=pltpu.CompilerParams(
            vmem_limit_bytes=56 * 1024 * 1024, collective_id=0, has_side_effects=True
        ),
    )(
        coords,
        solution,
        residual,
        direction,
        order.reshape(blocks, LANES),
        leaf_skel,
        local_skel,
        upper_skel,
    )


def solution(mesh):
    in_specs = (
        P(None, "leaf"),
        P(None, "leaf"),
        P(None, "leaf"),
        P(None, "leaf"),
        P("leaf"),
        P("leaf", None),
        P("leaf", None),
        P(None, "leaf", None),
    )
    out_specs = (P(None, "leaf"), P(None, "leaf"), P(None, "leaf"))
    return jax.shard_map(
        per_device, mesh=mesh, in_specs=in_specs, out_specs=out_specs, check_vma=False
    )
```

```python
import math

import jax
import jax.numpy as jnp
from jax import lax
from jax.experimental import pallas as pl
from jax.experimental.pallas import tpu as pltpu
from jax.sharding import PartitionSpec as P

ITERS = 4
MESH = pl.DeviceIdType.MESH
LANES = 128
LOG2E = math.log2(math.e)
F32 = jnp.float32
BF16 = jnp.bfloat16
VMEM = pl.BlockSpec(memory_space=pltpu.VMEM)

OWN0, OWN1, OWN2, OWN3, UP0, UP1, SIB, COUSIN, UNCLE = range(9)
PER_ROUND = 9


def pick(sources, index_row, first_block, block_count):
    low = index_row & (LANES - 1)
    high = index_row >> 7
    outs = [None] * len(sources)
    for block in range(block_count):
        hit = None
        for n, source in enumerate(sources):
            held = source(first_block + block)
            rows = held.shape[0]
            place = jnp.broadcast_to(low, (rows, LANES))
            got = jnp.take_along_axis(held, place, axis=1, mode="promise_in_bounds")
            if outs[n] is None:
                outs[n] = got
            else:
                hit = jnp.broadcast_to(high, (rows, LANES)) == block
                outs[n] = jnp.where(hit, got, outs[n])
    return outs


def block_of(ref):
    return lambda b: ref[:, b * LANES : (b + 1) * LANES]


def split(value):
    high = value.astype(BF16)
    return high, (value - high.astype(F32)).astype(BF16)


def split3(value):
    high = value.astype(BF16)
    rest = value - high.astype(F32)
    mid = rest.astype(BF16)
    return high, mid, (rest - mid.astype(F32)).astype(BF16)


def mm(a, b):
    return jnp.dot(a, b, preferred_element_type=F32)


def mm_t(a, b):
    return lax.dot_general(a, b, (((1,), (1,)), ((), ())), preferred_element_type=F32)


def stack3(value):
    return jnp.concatenate(split3(value), axis=0)


def fold3(wide):
    rows = wide.shape[0] // 3
    return wide[:rows] + (wide[rows : 2 * rows] + wide[2 * rows :])


def norm_rows(norms, first):
    high, mid, low = (part.astype(F32) for part in split3(norms))
    shape = (16, norms.shape[1])
    row = lax.broadcasted_iota(jnp.int32, shape, 0)
    one = jnp.where((row >= 3 - first) & (row < 6 - first), 1.0, 0.0)
    tile = jnp.where(row == first, high, one)
    tile = jnp.where(row == first + 1, mid, tile)
    return jnp.where(row == first + 2, low, tile)


def left_form(points):
    high, mid, low = (part.astype(F32) for part in split3(points))
    norms = jnp.sum(points * points, axis=0, keepdims=True) * (-LOG2E / 32.0)
    extra = norm_rows(norms, 0)
    full = jnp.concatenate([high, high, mid, mid, high, low, extra, jnp.zeros_like(extra)], axis=0)
    return jnp.transpose(full, (1, 0)).astype(BF16)


def right_form(points):
    high, mid, low = split3(points * (LOG2E / 16.0))
    norms = jnp.sum(points * points, axis=0, keepdims=True) * (-LOG2E / 32.0)
    extra = norm_rows(norms, 3).astype(BF16)
    return jnp.concatenate([high, mid, high, mid, low, high, extra, jnp.zeros_like(extra)], axis=0)


def softmax2(scores, axis):
    weights = jnp.exp2(scores - jnp.max(scores, axis=axis, keepdims=True))
    return weights * (1.0 / jnp.sum(weights, axis=axis, keepdims=True))


def row_dot(a, b):
    return jnp.sum(a * b, axis=1, keepdims=True)


def finish_state(x_in, gain, r_in, p_in, ratio, x_out, r_out, p_out):
    x_out[...] = x_in[...] + gain[...]
    r_out[...] = r_in[...]
    p_out[...] = r_in[...] + ratio[:, 0:1] * p_in[...]


def solve(coords, r_in, p_in, order, leaf_skel, local_skel, upper, x_out, r_out, p_out, ratio,
          near_mat, lefts, rights, ut_hi, ut_lo, t_hi, t_lo, pts, vec, vsplit, image, q_ref, r_ref, p_ref, gain,
          digits, marks, inverse, skel, parent, state, cps,
          points_out, points_in, coef_out, coef_in, sums_out, sums_in, middles, coefs, line_out, line_in, plane_out, plane_in,
          send_sem, recv_sem, sums_send, sums_recv, line_send, line_recv, plane_send, plane_recv):
    me = lax.axis_index("leaf")
    rounds = 4
    line = 16
    leaves, leaf_size = near_mat.shape[0], near_mat.shape[1]
    scale = 1.0 / leaf_size
    rank = parent.shape[1]
    rhs = vec.shape[0]
    local = rounds * PER_ROUND
    blocks = order.shape[0]
    bits = [(me // (1 << u)) % 2 for u in range(2 * rounds)]

    def partner(g, t):
        step = 1 << (2 * g)
        low = (1 - 2 * bits[2 * g]) * step
        high = (1 - 2 * bits[2 * g + 1]) * (2 * step)
        return me + (t % 2) * low + (t // 2) * high

    def on_line(t):
        return me + sum((1 - 2 * bits[u]) * (1 << u) for u in range(4) if t >> u & 1)

    def on_plane(t):
        return me + sum((1 - 2 * bits[u + 4]) * (1 << (u + 4)) for u in range(4) if t >> u & 1)

    barrier = pltpu.get_barrier_semaphore()
    for t in range(1, line):
        pl.semaphore_signal(barrier, inc=1, device_id=(on_line(t),), device_id_type=MESH)
        pl.semaphore_signal(barrier, inc=1, device_id=(on_plane(t),), device_id_type=MESH)

    def copies(src, dst, sent, received, g):
        return [
            pltpu.make_async_remote_copy(
                src_ref=src,
                dst_ref=dst.at[t - 1],
                send_sem=sent.at[t - 1],
                recv_sem=received.at[t - 1],
                device_id=(partner(g, t),),
                device_id_type=MESH,
            )
            for t in range(1, 4)
        ]

    def line_copies(phase):
        return [
            pltpu.make_async_remote_copy(
                src_ref=line_out,
                dst_ref=line_in.at[phase, t - 1],
                send_sem=line_send.at[t - 1],
                recv_sem=line_recv.at[phase, t - 1],
                device_id=(on_line(t),),
                device_id_type=MESH,
            )
            for t in range(1, line)
        ]

    def plane_copies(phase):
        return [
            pltpu.make_async_remote_copy(
                src_ref=plane_out,
                dst_ref=plane_in.at[phase, t - 1],
                send_sem=plane_send.at[t - 1],
                recv_sem=plane_recv.at[phase, t - 1],
                device_id=(on_plane(t),),
                device_id_type=MESH,
            )
            for t in range(1, line)
        ]

    tile_lane = lax.broadcasted_iota(jnp.int32, (8, LANES), 1)

    def to_tile(*columns):
        tile = jnp.zeros((8, LANES), F32)
        for n, column in enumerate(columns):
            tile = jnp.where(tile_lane == 2 * n, column[0:8], tile)
            tile = jnp.where(tile_lane == 2 * n + 1, column[8:16], tile)
        return tile

    def from_tile(tile, n=0):
        return jnp.concatenate([tile[:, 2 * n : 2 * n + 1], tile[:, 2 * n + 1 : 2 * n + 2]], axis=0)

    def line_sum(own, got):
        parts = [own[...]] + [got[t] for t in range(line - 1)]
        while len(parts) > 1:
            parts = [a + b for a, b in zip(parts[0::2], parts[1::2])]
        return parts[0]

    def keep(slot, value):
        high, low = split(value)
        t_hi[slot] = high
        t_lo[slot] = low

    def times(stacked, slot):
        return fold3(mm(stacked, t_hi[slot]) + mm(stacked, t_lo[slot]))

    def times_t(stacked, slot):
        return fold3(mm_t(stacked, t_hi[slot]) + mm_t(stacked, t_lo[slot]))

    def choose(first_is_own, index_row, own, other):
        swapped = jnp.where(index_row >= rank, index_row - rank, index_row + rank)
        want = jnp.where(first_is_own, index_row, swapped)
        place = lax.broadcasted_iota(jnp.int32, (rank, rank), 0).astype(F32)
        got = None
        for n, points in enumerate((own, other)):
            hot = jnp.where(place + float(n * rank) == want, 1.0, 0.0).astype(BF16)
            part = fold3(mm(stack3(points), hot))
            got = part if got is None else got + part
        return got

    def place_points(ob, carry):
        row = order[pl.ds(ob, 1), :]
        span = pl.ds(pl.multiple_of(ob * LANES, LANES), LANES)
        pts[:, span] = pick([block_of(coords)], row, 0, blocks)[0]
        place = ob * LANES + lax.broadcasted_iota(jnp.int32, (blocks, LANES), 1)
        hit = lax.broadcasted_iota(jnp.int32, (blocks, LANES), 0) == (row >> 7)
        digits[0:blocks, span] = jnp.where(hit, (place >> 5).astype(F32), 0.0).astype(BF16)
        digits[blocks : 2 * blocks, span] = jnp.where(hit, (place & 31).astype(F32), 0.0).astype(BF16)
        lane_hit = lax.broadcasted_iota(jnp.int32, (LANES, LANES), 0) == (row & (LANES - 1))
        marks[:, span] = jnp.where(lane_hit, 1.0, 0.0).astype(BF16)
        return carry

    lax.fori_loop(0, blocks // 4, lambda group, carry: [place_points(group * 4 + n, carry) for n in range(4)][-1], 0)
    leaf_blocks = blocks // leaves
    per = rank // LANES
    for leaf in range(leaves):
        for ob in range(per):
            row = leaf_skel[leaf : leaf + 1, ob * LANES : (ob + 1) * LANES]
            (got,) = pick([block_of(pts)], row, leaf * leaf_blocks, leaf_blocks)
            skel[leaf, :, ob * LANES : (ob + 1) * LANES] = got
    both = lambda b: skel[b // per, :, (b % per) * LANES : (b % per + 1) * LANES]
    for ob in range(per):
        row = local_skel[0:1, ob * LANES : (ob + 1) * LANES]
        (got,) = pick([both], row, 0, 2 * per)
        parent[:, ob * LANES : (ob + 1) * LANES] = got
    pl.semaphore_wait(barrier, 2 * (line - 1))

    def place_state(source, target):
        def body(group, carry):
            for n in range(4):
                ob = group * 4 + n
                span = pl.ds(pl.multiple_of(ob * LANES, LANES), LANES)
                target[:, span] = pick([block_of(source)], order[pl.ds(ob, 1), :], 0, blocks)[0]
            return carry

        lax.fori_loop(0, blocks // 4, body, 0)

    def invert():
        found = mm_t(digits[...], marks[...])
        inverse[...] = (found[0:blocks] * 32.0 + found[blocks : 2 * blocks]).astype(jnp.int32)

    def make_near():
        for leaf in range(leaves):
            cols = slice(leaf * leaf_size, (leaf + 1) * leaf_size)
            lefts[leaf] = left_form(pts[:, cols])
            rights[:, cols] = right_form(pts[:, cols])

            def body(j, carry, leaf=leaf, cols=cols):
                span = pl.ds(pl.multiple_of(j * rank, rank), rank)
                near_mat[leaf, span, :] = jnp.exp2(mm(lefts[leaf, span, :], rights[:, cols])).astype(BF16)
                return carry

            lax.fori_loop(0, leaf_size // rank, body, 0)

    def make_basis(leaf):
        left = left_form(skel[leaf])

        def body(group, carry):
            for n in range(4):
                j = group * 4 + n
                inner = pl.ds(pl.multiple_of(j * rank, rank), rank)
                span = pl.ds(pl.multiple_of(leaf * leaf_size + j * rank, rank), rank)
                high, low = split(softmax2(mm(left, rights[:, span]), 0))
                ut_hi[leaf, :, inner] = high
                ut_lo[leaf, :, inner] = low
            return carry

        lax.fori_loop(0, leaf_size // rank // 4, body, 0)

    def make_local():
        skel_left = [left_form(skel[leaf]) for leaf in range(leaves)]
        parent_right = right_form(parent[...])
        for leaf in range(leaves):
            keep(local + leaf, softmax2(mm(skel_left[leaf], parent_right), 1))
        keep(local + 2, jnp.exp2(mm(skel_left[0], right_form(skel[1]))) * scale)

    def make_gram():
        for leaf in range(leaves):
            high, low = ut_hi[leaf], ut_lo[leaf]
            cross = mm_t(high, low)
            keep(local + 3 + leaf, mm_t(high, high) + (cross + jnp.transpose(cross, (1, 0))))

    def make_round(g):
        base = g * PER_ROUND
        low = [points_out[g, 0:16, :]] + [points_in[g, t, 0:16, :] for t in range(3)]
        mids = [middles[g, n] for n in range(2)]
        low_left = [left_form(x) for x in low]
        mid_left = [left_form(x) for x in mids]
        mid_right = [right_form(x) for x in mids]
        for t in range(4):
            keep(base + OWN0 + t, softmax2(mm(low_left[t], mid_right[t // 2]), 1))
        keep(base + SIB, jnp.exp2(mm(low_left[1], right_form(low[0]))) * scale)
        keep(base + COUSIN, jnp.exp2(mm(low_left[3], right_form(low[2]))) * scale)
        keep(base + UNCLE, jnp.exp2(mm(mid_left[1], mid_right[0])) * scale)
        if g + 1 < rounds:
            top_right = right_form(points_out[g + 1, 0:16, :])
            for n in range(2):
                keep(base + UP0 + n, softmax2(mm(mid_left[n], top_right), 1))

    beside = [
        (lambda: place_state(p_in, vec),),
        (make_near,),
        (lambda: make_basis(0), lambda: make_round(0)),
        (lambda: make_basis(1), lambda: make_round(1), make_local),
    ]
    own = parent[...]
    for g in range(rounds):
        u = 2 * g
        points_out[g, 0:16, :] = own
        points_out[g, 16:24, :] = jnp.broadcast_to(upper[u].astype(F32), (8, rank))
        sends = copies(points_out.at[g], points_in.at[g], send_sem.at[g], recv_sem.at[0, g], g)
        for t in (2, 3, 1):
            sends[t - 1].start()
        for work in beside[g]:
            work()
        for c in sends:
            c.wait()
        low = [own] + [points_in[g, t, 0:16, :] for t in range(3)]
        lists = [points_out[g, 16:17, :], points_in[g, 1, 16:17, :]]
        mids = [choose(bits[u] == 0, lists[n], low[2 * n], low[2 * n + 1]) for n in range(2)]
        for n in range(2):
            middles[g, n] = mids[n]
        if g + 1 < rounds:
            own = choose(bits[u + 1] == 0, upper[u + 1].astype(F32), mids[0], mids[1])

    p_ref[...] = jnp.zeros_like(p_ref)
    q_ref[...] = jnp.zeros_like(q_ref)
    gain[...] = jnp.zeros_like(gain)
    state[0] = jnp.ones(state.shape[1:], F32)
    for n in range(1, state.shape[0]):
        state[n] = jnp.zeros(state.shape[1:], F32)
    lane = lax.broadcasted_iota(jnp.int32, (rhs, LANES), 1)
    OF_V, OF_R, OF_P, OF_Q, OF_NEAR, DOWN = range(6)

    def columns(leaf):
        return slice(leaf * leaf_size, (leaf + 1) * leaf_size)

    def leaf_up(ref, leaf):
        part = stack3(ref[:, columns(leaf)])
        return fold3(mm_t(part, ut_hi[leaf]) + mm_t(part, ut_lo[leaf]))

    def near_product(leaf, first, last):
        def body(j, carry):
            inner = pl.ds(pl.multiple_of(j * rank, rank), rank)
            span = pl.ds(pl.multiple_of(leaf * leaf_size + j * rank, rank), rank)
            wide = fold3(mm(vsplit[:, columns(leaf)], near_mat[leaf, :, inner]))
            image[:, span] = 0.5 * vec[:, span] + wide * scale
            return carry

        lax.fori_loop(first, last, body, 0)

    def finish():
        alpha, beta, guess = (state[n, :, 0:1] for n in (3, 4, 2))
        for leaf in range(leaves):
            cols = columns(leaf)
            part = stack3(coefs[DOWN, leaf])
            full = image[:, cols] + fold3(mm(part, ut_hi[leaf]) + mm(part, ut_lo[leaf]))
            p_new = vec[:, cols] + beta * p_ref[:, cols]
            q_new = full + beta * q_ref[:, cols]
            p_ref[:, cols] = p_new
            q_ref[:, cols] = q_new
            gain[:, cols] += alpha * p_new
            r_new = r_ref[:, cols] - alpha * q_new
            r_ref[:, cols] = r_new
            vec[:, cols] = r_new + guess * p_new

    for leaf in range(leaves):
        coefs[OF_V, leaf] = leaf_up(vec, leaf)
        coefs[OF_P, leaf] = jnp.zeros(coefs.shape[2:], F32)
        coefs[OF_Q, leaf] = jnp.zeros(coefs.shape[2:], F32)
    chunks = leaf_size // rank

    def iteration(k, carry):
        leaf_coef = [coefs[OF_V, leaf] for leaf in range(leaves)]
        wide = [stack3(x) for x in leaf_coef]
        coef = times(wide[0], local) + times(wide[1], local + 1)
        last = None
        for g in range(rounds):
            base = g * PER_ROUND
            coef_out[g] = coef
            sends = copies(coef_out.at[g], coef_in.at[k, g], send_sem.at[g], recv_sem.at[1 + k, g], g)
            for t in (2, 3, 1):
                sends[t - 1].start()
            if g == 0:
                leaf_cp = [times_t(wide[1], local + 2), times(wide[0], local + 2)]
                sums = jnp.where(lane == 2, 2.0 * row_dot(leaf_coef[0], leaf_cp[0]), 0.0)
            else:
                sums = last()
            sums_out[g] = sums
            sum_sends = copies(sums_out.at[g], sums_in.at[k, g], sums_send.at[g], sums_recv.at[k, g], g)
            for c in sum_sends:
                c.start()
            if g == 0:
                pl.when(k > 0)(finish)
                pl.when(k == 0)(lambda: place_state(r_in, r_ref))
                vsplit[...] = stack3(vec[...])
                near_product(0, 0, chunks // 4)
            if g == 1:
                near_product(0, chunks // 4, chunks)
                near_product(1, 0, chunks)
                line_out[...] = to_tile(
                    row_dot(vec[...], image[...]),
                    row_dot(r_ref[...], r_ref[...]),
                    row_dot(vec[...], q_ref[...]),
                    row_dot(r_ref[...], vec[...]),
                    row_dot(vec[...], vec[...]),
                )
                side = line_copies(k)
                for c in side:
                    c.start()
            if g == 2:
                for leaf in range(leaves):
                    coefs[OF_NEAR, leaf] = leaf_up(image, leaf)
            if g == 3:
                for c in side:
                    c.wait()
                plane_out[...] = line_sum(line_out, line_in.at[k])
                side = plane_copies(k)
                for c in side:
                    c.start()
            if g > 0:

                @pl.when(k == 0)
                def _(g=g):
                    if g < 3:
                        make_round(g + 1)
                    else:
                        make_gram()
                        invert()
                        for leaf in range(leaves):
                            coefs[OF_R, leaf] = leaf_up(r_ref, leaf)

            got = [coef] + [None] * 3
            wide = [stack3(coef)] + [None] * 3
            moved = [times(wide[0], base + OWN0)] + [None] * 3
            for t in (1, 3, 2):
                sends[t - 1].wait()
                got[t] = coef_in[k, g, t - 1]
                wide[t] = stack3(got[t])
                moved[t] = times(wide[t], base + OWN0 + t)
                if t == 1:
                    mid0 = moved[0] + moved[1]
                    if g + 1 < rounds:
                        up0 = times(stack3(mid0), base + UP0)
            mid1 = moved[2] + moved[3]
            mid1_wide = stack3(mid1)
            if g + 1 < rounds:
                coef = up0 + times(mid1_wide, base + UP1)

            def last(g=g, base=base, got=got, wide=wide, mid0=mid0, mid1_wide=mid1_wide, sums=sums, sent=sum_sends):
                low_cp = times(wide[1], base + SIB)
                mid_cp = times(mid1_wide, base + UNCLE)
                cps[2 * g] = low_cp
                cps[2 * g + 1] = mid_cp
                quad = row_dot(got[0], low_cp) + row_dot(got[2], times(wide[3], base + COUSIN)) + row_dot(mid0, mid_cp)
                for c in sent:
                    c.wait()
                far = [sums_in[k, g, t] for t in range(3)]
                return (sums + far[0]) + (far[1] + far[2]) + jnp.where(lane == 2, 2.0 * quad, 0.0)

        sums = last()
        down = cps[2 * rounds - 1]
        for u in range(2 * rounds - 2, -1, -1):
            down = cps[u] + times_t(stack3(down), (u // 2) * PER_ROUND + (UP0 if u % 2 else OWN0))
        down_wide = stack3(down)
        image_coef = []
        for leaf in range(leaves):
            leaf_down = leaf_cp[leaf] + times_t(down_wide, local + leaf)
            coefs[DOWN, leaf] = leaf_down
            image_coef.append(coefs[OF_NEAR, leaf] + times(stack3(leaf_down), local + 3 + leaf))
        for c in side:
            c.wait()
        tile = line_sum(plane_out, plane_in.at[k])
        near, fresh, cross, with_v, of_v = (from_tile(tile, n) for n in range(5))
        beta = fresh / state[0, :, 0:1] - state[2, :, 0:1]
        guess = jnp.where(k == 0, 1.0 + (fresh - 2.0 * with_v) / of_v, 0.0)
        curve = (sums[:, 2:3] + near) + 2.0 * beta * cross + beta * beta * state[1, :, 0:1]
        alpha = fresh / curve
        for n, column in enumerate((fresh, curve, guess, alpha, beta)):
            state[n] = jnp.broadcast_to(column, (rhs, LANES))
        for leaf in range(leaves):
            p_coef = coefs[OF_V, leaf] + beta * coefs[OF_P, leaf]
            q_coef = image_coef[leaf] + beta * coefs[OF_Q, leaf]
            r_coef = coefs[OF_R, leaf] - alpha * q_coef
            coefs[OF_P, leaf] = p_coef
            coefs[OF_Q, leaf] = q_coef
            coefs[OF_R, leaf] = r_coef
            coefs[OF_V, leaf] = r_coef + guess * p_coef
        return carry

    lax.fori_loop(0, ITERS, iteration, 0)
    finish()

    sources = [block_of(gain), block_of(r_ref), block_of(p_ref)]

    def restore(group, carry):
        for n in range(4):
            ob = group * 4 + n
            span = pl.ds(pl.multiple_of(ob * LANES, LANES), LANES)
            got = pick(sources, inverse[pl.ds(ob, 1), :], 0, blocks)
            x_out[:, span] = got[0]
            r_out[:, span] = got[1]
            p_out[:, span] = got[2]
        return carry

    line_out[...] = to_tile(row_dot(r_ref[...], r_ref[...]))
    sends = line_copies(ITERS)
    for c in sends:
        c.start()
    lax.fori_loop(0, blocks // 8, restore, 0)
    for c in sends:
        c.wait()
    plane_out[...] = line_sum(line_out, line_in.at[ITERS])
    sends = plane_copies(ITERS)
    for c in sends:
        c.start()
    lax.fori_loop(blocks // 8, blocks // 4, restore, 0)
    for c in sends:
        c.wait()
    tile = line_sum(plane_out, plane_in.at[ITERS])
    ratio[...] = jnp.broadcast_to(from_tile(tile) / state[0, :, 0:1], ratio.shape)


def per_device(coords, solution, residual, direction, order, leaf_skel, local_skel, upper_skel):
    dims, count = coords.shape
    rhs = solution.shape[0]
    leaves, rank = leaf_skel.shape
    leaf_size = count // leaves
    blocks = count // LANES
    flat = jax.ShapeDtypeStruct((rhs, count), F32)
    slots = 4 * PER_ROUND + 5
    gain, resid, search, ratio = pl.pallas_call(
        solve,
        out_shape=(flat, flat, flat, jax.ShapeDtypeStruct((rhs, LANES), F32)),
        in_specs=[VMEM] * 7,
        out_specs=(VMEM,) * 4,
        scratch_shapes=[
            pltpu.VMEM((leaves, leaf_size, leaf_size), BF16),
            pltpu.VMEM((leaves, leaf_size, LANES), BF16),
            pltpu.VMEM((LANES, count), BF16),
            pltpu.VMEM((leaves, rank, leaf_size), BF16),
            pltpu.VMEM((leaves, rank, leaf_size), BF16),
            pltpu.VMEM((slots, rank, rank), BF16),
            pltpu.VMEM((slots, rank, rank), BF16),
            pltpu.VMEM((dims, count), F32),
            pltpu.VMEM((rhs, count), F32),
            pltpu.VMEM((3 * rhs, count), BF16),
            pltpu.VMEM((rhs, count), F32),
            pltpu.VMEM((rhs, count), F32),
            pltpu.VMEM((rhs, count), F32),
            pltpu.VMEM((rhs, count), F32),
            pltpu.VMEM((rhs, count), F32),
            pltpu.VMEM((2 * blocks, count), BF16),
            pltpu.VMEM((LANES, count), BF16),
            pltpu.VMEM((blocks, LANES), jnp.int32),
            pltpu.VMEM((leaves, dims, rank), F32),
            pltpu.VMEM((dims, rank), F32),
            pltpu.VMEM((5, rhs, LANES), F32),
            pltpu.VMEM((8, rhs, rank), F32),
            pltpu.VMEM((4, dims + 8, rank), F32),
            pltpu.VMEM((4, 3, dims + 8, rank), F32),
            pltpu.VMEM((4, rhs, rank), F32),
            pltpu.VMEM((ITERS, 4, 3, rhs, rank), F32),
            pltpu.VMEM((4, rhs, LANES), F32),
            pltpu.VMEM((ITERS, 4, 3, rhs, LANES), F32),
            pltpu.VMEM((4, 2, dims, rank), F32),
            pltpu.VMEM((6, leaves, rhs, rank), F32),
            pltpu.VMEM((8, LANES), F32),
            pltpu.VMEM((ITERS + 1, 15, 8, LANES), F32),
            pltpu.VMEM((8, LANES), F32),
            pltpu.VMEM((ITERS + 1, 15, 8, LANES), F32),
            pltpu.SemaphoreType.DMA((4, 3)),
            pltpu.SemaphoreType.DMA((ITERS + 1, 4, 3)),
            pltpu.SemaphoreType.DMA((4, 3)),
            pltpu.SemaphoreType.DMA((ITERS, 4, 3)),
            pltpu.SemaphoreType.DMA((15,)),
            pltpu.SemaphoreType.DMA((ITERS + 1, 15)),
            pltpu.SemaphoreType.DMA((15,)),
            pltpu.SemaphoreType.DMA((ITERS + 1, 15)),
        ],
        compiler_params=pltpu.CompilerParams(
            vmem_limit_bytes=56 * 1024 * 1024, collective_id=0, has_side_effects=True
        ),
    )(
        coords,
        residual,
        direction,
        order.reshape(blocks, LANES),
        leaf_skel,
        local_skel,
        upper_skel,
    )
    return pl.pallas_call(
        finish_state,
        out_shape=(flat, flat, flat),
        in_specs=[VMEM] * 5,
        out_specs=(VMEM,) * 3,
    )(solution, gain, resid, search, ratio)


def solution(mesh):
    in_specs = (
        P(None, "leaf"),
        P(None, "leaf"),
        P(None, "leaf"),
        P(None, "leaf"),
        P("leaf"),
        P("leaf", None),
        P("leaf", None),
        P(None, "leaf", None),
    )
    out_specs = (P(None, "leaf"), P(None, "leaf"), P(None, "leaf"))
    return jax.shard_map(
        per_device, mesh=mesh, in_specs=in_specs, out_specs=out_specs, check_vma=False
    )
```

```python
import math

import jax
import jax.numpy as jnp
from jax import lax
from jax.experimental import pallas as pl
from jax.experimental.pallas import tpu as pltpu
from jax.sharding import PartitionSpec as P

ITERS = 4
MESH = pl.DeviceIdType.MESH
LANES = 128
LOG2E = math.log2(math.e)
F32 = jnp.float32
BF16 = jnp.bfloat16
VMEM = pl.BlockSpec(memory_space=pltpu.VMEM)

OWN0, OWN1, OWN2, OWN3, UP0, UP1, SIB, COUSIN, UNCLE = range(9)
PER_ROUND = 9

LINE_ORDER = (8, 9, 10, 11, 6, 7, 14, 15, 4, 5, 12, 13, 2, 3, 1)
PLANE_ORDER = (10, 6, 14, 9, 11, 5, 7, 13, 15, 2, 8, 1, 3, 4, 12)


def pick(sources, index_row, first_block, block_count):
    low = index_row & (LANES - 1)
    high = index_row >> 7
    outs = [None] * len(sources)
    for block in range(block_count):
        hit = None
        for n, source in enumerate(sources):
            held = source(first_block + block)
            rows = held.shape[0]
            place = jnp.broadcast_to(low, (rows, LANES))
            got = jnp.take_along_axis(held, place, axis=1, mode="promise_in_bounds")
            if outs[n] is None:
                outs[n] = got
            else:
                hit = jnp.broadcast_to(high, (rows, LANES)) == block
                outs[n] = jnp.where(hit, got, outs[n])
    return outs


def block_of(ref):
    return lambda b: ref[:, b * LANES : (b + 1) * LANES]


def split(value):
    high = value.astype(BF16)
    return high, (value - high.astype(F32)).astype(BF16)


def split3(value):
    high = value.astype(BF16)
    rest = value - high.astype(F32)
    mid = rest.astype(BF16)
    return high, mid, (rest - mid.astype(F32)).astype(BF16)


def mm(a, b):
    return jnp.dot(a, b, preferred_element_type=F32)


def mm_t(a, b):
    return lax.dot_general(a, b, (((1,), (1,)), ((), ())), preferred_element_type=F32)


def stack3(value):
    return jnp.concatenate(split3(value), axis=0)


def fold3(wide):
    rows = wide.shape[0] // 3
    return wide[:rows] + (wide[rows : 2 * rows] + wide[2 * rows :])


def norm_rows(norms, first):
    high, mid, low = (part.astype(F32) for part in split3(norms))
    shape = (16, norms.shape[1])
    row = lax.broadcasted_iota(jnp.int32, shape, 0)
    one = jnp.where((row >= 3 - first) & (row < 6 - first), 1.0, 0.0)
    tile = jnp.where(row == first, high, one)
    tile = jnp.where(row == first + 1, mid, tile)
    return jnp.where(row == first + 2, low, tile)


def left_form(points):
    high, mid, low = (part.astype(F32) for part in split3(points))
    norms = jnp.sum(points * points, axis=0, keepdims=True) * (-LOG2E / 32.0)
    extra = norm_rows(norms, 0)
    full = jnp.concatenate([high, high, mid, mid, high, low, extra, jnp.zeros_like(extra)], axis=0)
    return jnp.transpose(full, (1, 0)).astype(BF16)


def right_form(points):
    high, mid, low = split3(points * (LOG2E / 16.0))
    norms = jnp.sum(points * points, axis=0, keepdims=True) * (-LOG2E / 32.0)
    extra = norm_rows(norms, 3).astype(BF16)
    return jnp.concatenate([high, mid, high, mid, low, high, extra, jnp.zeros_like(extra)], axis=0)


def softmax2(scores, axis):
    weights = jnp.exp2(scores - jnp.max(scores, axis=axis, keepdims=True))
    return weights * (1.0 / jnp.sum(weights, axis=axis, keepdims=True))


def row_dot(a, b):
    return jnp.sum(a * b, axis=1, keepdims=True)


def finish_state(x_in, gain, r_in, p_in, ratio, x_out, r_out, p_out):
    x_out[...] = x_in[...] + gain[...]
    r_out[...] = r_in[...]
    p_out[...] = r_in[...] + ratio[:, 0:1] * p_in[...]


def solve(coords, r_in, p_in, order, leaf_skel, local_skel, upper, x_out, r_out, p_out, ratio,
          near_mat, lefts, rights, ut_hi, ut_lo, t_hi, t_lo, pts, vec, vsplit, image, q_ref, r_ref, p_ref, gain,
          digits, marks, inverse, skel, parent, state, cps,
          points_out, points_in, coef_out, coef_in, sums_out, sums_in, middles, coefs, line_out, line_in, plane_out, plane_in,
          send_sem, recv_sem, sums_send, sums_recv, line_send, line_recv, plane_send, plane_recv):
    me = lax.axis_index("leaf")
    rounds = 4
    line = 16
    leaves, leaf_size = near_mat.shape[0], near_mat.shape[1]
    scale = 1.0 / leaf_size
    rank = parent.shape[1]
    rhs = vec.shape[0]
    local = rounds * PER_ROUND
    blocks = order.shape[0]
    bits = [(me // (1 << u)) % 2 for u in range(2 * rounds)]

    def partner(g, t):
        step = 1 << (2 * g)
        low = (1 - 2 * bits[2 * g]) * step
        high = (1 - 2 * bits[2 * g + 1]) * (2 * step)
        return me + (t % 2) * low + (t // 2) * high

    def on_line(t):
        return me + sum((1 - 2 * bits[u]) * (1 << u) for u in range(4) if t >> u & 1)

    def on_plane(t):
        return me + sum((1 - 2 * bits[u + 4]) * (1 << (u + 4)) for u in range(4) if t >> u & 1)

    barrier = pltpu.get_barrier_semaphore()
    for t in range(1, line):
        pl.semaphore_signal(barrier, inc=1, device_id=(on_line(t),), device_id_type=MESH)
        pl.semaphore_signal(barrier, inc=1, device_id=(on_plane(t),), device_id_type=MESH)

    def copies(src, dst, sent, received, g):
        return [
            pltpu.make_async_remote_copy(
                src_ref=src,
                dst_ref=dst.at[t - 1],
                send_sem=sent.at[t - 1],
                recv_sem=received.at[t - 1],
                device_id=(partner(g, t),),
                device_id_type=MESH,
            )
            for t in range(1, 4)
        ]

    def line_copies(phase):
        return [
            pltpu.make_async_remote_copy(
                src_ref=line_out,
                dst_ref=line_in.at[phase, t - 1],
                send_sem=line_send.at[t - 1],
                recv_sem=line_recv.at[phase, t - 1],
                device_id=(on_line(t),),
                device_id_type=MESH,
            )
            for t in LINE_ORDER
        ]

    def plane_copies(phase):
        return [
            pltpu.make_async_remote_copy(
                src_ref=plane_out,
                dst_ref=plane_in.at[phase, t - 1],
                send_sem=plane_send.at[t - 1],
                recv_sem=plane_recv.at[phase, t - 1],
                device_id=(on_plane(t),),
                device_id_type=MESH,
            )
            for t in PLANE_ORDER
        ]

    tile_lane = lax.broadcasted_iota(jnp.int32, (8, LANES), 1)

    def to_tile(*columns):
        tile = jnp.zeros((8, LANES), F32)
        for n, column in enumerate(columns):
            tile = jnp.where(tile_lane == 2 * n, column[0:8], tile)
            tile = jnp.where(tile_lane == 2 * n + 1, column[8:16], tile)
        return tile

    def from_tile(tile, n=0):
        return jnp.concatenate([tile[:, 2 * n : 2 * n + 1], tile[:, 2 * n + 1 : 2 * n + 2]], axis=0)

    def line_sum(own, got):
        parts = [own[...]] + [got[t] for t in range(line - 1)]
        while len(parts) > 1:
            parts = [a + b for a, b in zip(parts[0::2], parts[1::2])]
        return parts[0]

    def keep(slot, value):
        high, low = split(value)
        t_hi[slot] = high
        t_lo[slot] = low

    def times(stacked, slot):
        return fold3(mm(stacked, t_hi[slot]) + mm(stacked, t_lo[slot]))

    def times_t(stacked, slot):
        return fold3(mm_t(stacked, t_hi[slot]) + mm_t(stacked, t_lo[slot]))

    def choose(first_is_own, index_row, own, other):
        swapped = jnp.where(index_row >= rank, index_row - rank, index_row + rank)
        want = jnp.where(first_is_own, index_row, swapped)
        place = lax.broadcasted_iota(jnp.int32, (rank, rank), 0).astype(F32)
        got = None
        for n, points in enumerate((own, other)):
            hot = jnp.where(place + float(n * rank) == want, 1.0, 0.0).astype(BF16)
            part = fold3(mm(stack3(points), hot))
            got = part if got is None else got + part
        return got

    def place_points(ob, carry):
        row = order[pl.ds(ob, 1), :]
        span = pl.ds(pl.multiple_of(ob * LANES, LANES), LANES)
        pts[:, span] = pick([block_of(coords)], row, 0, blocks)[0]
        place = ob * LANES + lax.broadcasted_iota(jnp.int32, (blocks, LANES), 1)
        hit = lax.broadcasted_iota(jnp.int32, (blocks, LANES), 0) == (row >> 7)
        digits[0:blocks, span] = jnp.where(hit, (place >> 5).astype(F32), 0.0).astype(BF16)
        digits[blocks : 2 * blocks, span] = jnp.where(hit, (place & 31).astype(F32), 0.0).astype(BF16)
        lane_hit = lax.broadcasted_iota(jnp.int32, (LANES, LANES), 0) == (row & (LANES - 1))
        marks[:, span] = jnp.where(lane_hit, 1.0, 0.0).astype(BF16)
        return carry

    lax.fori_loop(0, blocks // 4, lambda group, carry: [place_points(group * 4 + n, carry) for n in range(4)][-1], 0)
    leaf_blocks = blocks // leaves
    per = rank // LANES
    for leaf in range(leaves):
        for ob in range(per):
            row = leaf_skel[leaf : leaf + 1, ob * LANES : (ob + 1) * LANES]
            (got,) = pick([block_of(pts)], row, leaf * leaf_blocks, leaf_blocks)
            skel[leaf, :, ob * LANES : (ob + 1) * LANES] = got
    both = lambda b: skel[b // per, :, (b % per) * LANES : (b % per + 1) * LANES]
    for ob in range(per):
        row = local_skel[0:1, ob * LANES : (ob + 1) * LANES]
        (got,) = pick([both], row, 0, 2 * per)
        parent[:, ob * LANES : (ob + 1) * LANES] = got
    pl.semaphore_wait(barrier, 2 * (line - 1))

    def place_state(source, target):
        def body(group, carry):
            for n in range(4):
                ob = group * 4 + n
                span = pl.ds(pl.multiple_of(ob * LANES, LANES), LANES)
                target[:, span] = pick([block_of(source)], order[pl.ds(ob, 1), :], 0, blocks)[0]
            return carry

        lax.fori_loop(0, blocks // 4, body, 0)

    def invert():
        found = mm_t(digits[...], marks[...])
        inverse[...] = (found[0:blocks] * 32.0 + found[blocks : 2 * blocks]).astype(jnp.int32)

    def make_near():
        for leaf in range(leaves):
            cols = slice(leaf * leaf_size, (leaf + 1) * leaf_size)
            lefts[leaf] = left_form(pts[:, cols])
            rights[:, cols] = right_form(pts[:, cols])

            def body(j, carry, leaf=leaf, cols=cols):
                span = pl.ds(pl.multiple_of(j * rank, rank), rank)
                near_mat[leaf, span, :] = jnp.exp2(mm(lefts[leaf, span, :], rights[:, cols])).astype(BF16)
                return carry

            lax.fori_loop(0, leaf_size // rank, body, 0)

    def make_basis(leaf):
        left = left_form(skel[leaf])

        def body(group, carry):
            for n in range(4):
                j = group * 4 + n
                inner = pl.ds(pl.multiple_of(j * rank, rank), rank)
                span = pl.ds(pl.multiple_of(leaf * leaf_size + j * rank, rank), rank)
                high, low = split(softmax2(mm(left, rights[:, span]), 0))
                ut_hi[leaf, :, inner] = high
                ut_lo[leaf, :, inner] = low
            return carry

        lax.fori_loop(0, leaf_size // rank // 4, body, 0)

    def make_local():
        skel_left = [left_form(skel[leaf]) for leaf in range(leaves)]
        parent_right = right_form(parent[...])
        for leaf in range(leaves):
            keep(local + leaf, softmax2(mm(skel_left[leaf], parent_right), 1))
        keep(local + 2, jnp.exp2(mm(skel_left[0], right_form(skel[1]))) * scale)

    def make_gram():
        for leaf in range(leaves):
            high, low = ut_hi[leaf], ut_lo[leaf]
            cross = mm_t(high, low)
            keep(local + 3 + leaf, mm_t(high, high) + (cross + jnp.transpose(cross, (1, 0))))

    def make_round(g):
        base = g * PER_ROUND
        low = [points_out[g, 0:16, :]] + [points_in[g, t, 0:16, :] for t in range(3)]
        mids = [middles[g, n] for n in range(2)]
        low_left = [left_form(x) for x in low]
        mid_left = [left_form(x) for x in mids]
        mid_right = [right_form(x) for x in mids]
        for t in range(4):
            keep(base + OWN0 + t, softmax2(mm(low_left[t], mid_right[t // 2]), 1))
        keep(base + SIB, jnp.exp2(mm(low_left[1], right_form(low[0]))) * scale)
        keep(base + COUSIN, jnp.exp2(mm(low_left[3], right_form(low[2]))) * scale)
        keep(base + UNCLE, jnp.exp2(mm(mid_left[1], mid_right[0])) * scale)
        if g + 1 < rounds:
            top_right = right_form(points_out[g + 1, 0:16, :])
            for n in range(2):
                keep(base + UP0 + n, softmax2(mm(mid_left[n], top_right), 1))

    beside = [
        (lambda: place_state(p_in, vec),),
        (make_near,),
        (lambda: make_basis(0), lambda: make_round(0)),
        (lambda: make_basis(1), lambda: make_round(1), make_local),
    ]
    own = parent[...]
    for g in range(rounds):
        u = 2 * g
        points_out[g, 0:16, :] = own
        points_out[g, 16:24, :] = jnp.broadcast_to(upper[u].astype(F32), (8, rank))
        sends = copies(points_out.at[g], points_in.at[g], send_sem.at[g], recv_sem.at[0, g], g)
        for t in (2, 3, 1):
            sends[t - 1].start()
        for work in beside[g]:
            work()
        for c in sends:
            c.wait()
        low = [own] + [points_in[g, t, 0:16, :] for t in range(3)]
        lists = [points_out[g, 16:17, :], points_in[g, 1, 16:17, :]]
        mids = [choose(bits[u] == 0, lists[n], low[2 * n], low[2 * n + 1]) for n in range(2)]
        for n in range(2):
            middles[g, n] = mids[n]
        if g + 1 < rounds:
            own = choose(bits[u + 1] == 0, upper[u + 1].astype(F32), mids[0], mids[1])

    p_ref[...] = jnp.zeros_like(p_ref)
    q_ref[...] = jnp.zeros_like(q_ref)
    gain[...] = jnp.zeros_like(gain)
    state[0] = jnp.ones(state.shape[1:], F32)
    for n in range(1, state.shape[0]):
        state[n] = jnp.zeros(state.shape[1:], F32)
    lane = lax.broadcasted_iota(jnp.int32, (rhs, LANES), 1)
    OF_V, OF_R, OF_P, OF_Q, OF_NEAR, DOWN = range(6)

    def columns(leaf):
        return slice(leaf * leaf_size, (leaf + 1) * leaf_size)

    def leaf_up(ref, leaf):
        part = stack3(ref[:, columns(leaf)])
        return fold3(mm_t(part, ut_hi[leaf]) + mm_t(part, ut_lo[leaf]))

    def near_product(leaf, first, last):
        def body(j, carry):
            inner = pl.ds(pl.multiple_of(j * rank, rank), rank)
            span = pl.ds(pl.multiple_of(leaf * leaf_size + j * rank, rank), rank)
            wide = fold3(mm(vsplit[:, columns(leaf)], near_mat[leaf, :, inner]))
            image[:, span] = 0.5 * vec[:, span] + wide * scale
            return carry

        lax.fori_loop(first, last, body, 0)

    def finish():
        alpha, beta, guess = (state[n, :, 0:1] for n in (3, 4, 2))
        for leaf in range(leaves):
            cols = columns(leaf)
            part = stack3(coefs[DOWN, leaf])
            full = image[:, cols] + fold3(mm(part, ut_hi[leaf]) + mm(part, ut_lo[leaf]))
            p_new = vec[:, cols] + beta * p_ref[:, cols]
            q_new = full + beta * q_ref[:, cols]
            p_ref[:, cols] = p_new
            q_ref[:, cols] = q_new
            gain[:, cols] += alpha * p_new
            r_new = r_ref[:, cols] - alpha * q_new
            r_ref[:, cols] = r_new
            vec[:, cols] = r_new + guess * p_new

    for leaf in range(leaves):
        coefs[OF_V, leaf] = leaf_up(vec, leaf)
        coefs[OF_P, leaf] = jnp.zeros(coefs.shape[2:], F32)
        coefs[OF_Q, leaf] = jnp.zeros(coefs.shape[2:], F32)
    chunks = leaf_size // rank

    def iteration(k, carry):
        leaf_coef = [coefs[OF_V, leaf] for leaf in range(leaves)]
        wide = [stack3(x) for x in leaf_coef]
        coef = times(wide[0], local) + times(wide[1], local + 1)
        last = None
        for g in range(rounds):
            base = g * PER_ROUND
            coef_out[g] = coef
            sends = copies(coef_out.at[g], coef_in.at[k, g], send_sem.at[g], recv_sem.at[1 + k, g], g)
            for t in (2, 3, 1):
                sends[t - 1].start()
            if g == 0:
                leaf_cp = [times_t(wide[1], local + 2), times(wide[0], local + 2)]
                sums = jnp.where(lane == 2, 2.0 * row_dot(leaf_coef[0], leaf_cp[0]), 0.0)
            else:
                sums = last()
            sums_out[g] = sums
            sum_sends = copies(sums_out.at[g], sums_in.at[k, g], sums_send.at[g], sums_recv.at[k, g], g)
            for c in sum_sends:
                c.start()
            if g == 0:
                pl.when(k > 0)(finish)
                pl.when(k == 0)(lambda: place_state(r_in, r_ref))
                vsplit[...] = stack3(vec[...])
                near_product(0, 0, chunks // 4)
            if g == 1:
                near_product(0, chunks // 4, chunks)
                near_product(1, 0, chunks)
                line_out[...] = to_tile(
                    row_dot(vec[...], image[...]),
                    row_dot(r_ref[...], r_ref[...]),
                    row_dot(vec[...], q_ref[...]),
                    row_dot(r_ref[...], vec[...]),
                    row_dot(vec[...], vec[...]),
                )
                side = line_copies(k)
                for c in side:
                    c.start()
            if g == 2:
                for leaf in range(leaves):
                    coefs[OF_NEAR, leaf] = leaf_up(image, leaf)
            if g == 3:
                for c in side:
                    c.wait()
                plane_out[...] = line_sum(line_out, line_in.at[k])
                side = plane_copies(k)
                for c in side:
                    c.start()
            if g > 0:

                @pl.when(k == 0)
                def _(g=g):
                    if g < 3:
                        make_round(g + 1)
                    else:
                        make_gram()
                        invert()
                        for leaf in range(leaves):
                            coefs[OF_R, leaf] = leaf_up(r_ref, leaf)

            got = [coef] + [None] * 3
            wide = [stack3(coef)] + [None] * 3
            moved = [times(wide[0], base + OWN0)] + [None] * 3
            for t in (1, 3, 2):
                sends[t - 1].wait()
                got[t] = coef_in[k, g, t - 1]
                wide[t] = stack3(got[t])
                moved[t] = times(wide[t], base + OWN0 + t)
                if t == 1:
                    mid0 = moved[0] + moved[1]
                    if g + 1 < rounds:
                        up0 = times(stack3(mid0), base + UP0)
            mid1 = moved[2] + moved[3]
            mid1_wide = stack3(mid1)
            if g + 1 < rounds:
                coef = up0 + times(mid1_wide, base + UP1)

            def last(g=g, base=base, got=got, wide=wide, mid0=mid0, mid1_wide=mid1_wide, sums=sums, sent=sum_sends):
                low_cp = times(wide[1], base + SIB)
                mid_cp = times(mid1_wide, base + UNCLE)
                cps[2 * g] = low_cp
                cps[2 * g + 1] = mid_cp
                quad = row_dot(got[0], low_cp) + row_dot(got[2], times(wide[3], base + COUSIN)) + row_dot(mid0, mid_cp)
                for c in sent:
                    c.wait()
                far = [sums_in[k, g, t] for t in range(3)]
                return (sums + far[0]) + (far[1] + far[2]) + jnp.where(lane == 2, 2.0 * quad, 0.0)

        sums = last()
        down = cps[2 * rounds - 1]
        for u in range(2 * rounds - 2, -1, -1):
            down = cps[u] + times_t(stack3(down), (u // 2) * PER_ROUND + (UP0 if u % 2 else OWN0))
        down_wide = stack3(down)
        image_coef = []
        for leaf in range(leaves):
            leaf_down = leaf_cp[leaf] + times_t(down_wide, local + leaf)
            coefs[DOWN, leaf] = leaf_down
            image_coef.append(coefs[OF_NEAR, leaf] + times(stack3(leaf_down), local + 3 + leaf))
        for c in side:
            c.wait()
        tile = line_sum(plane_out, plane_in.at[k])
        near, fresh, cross, with_v, of_v = (from_tile(tile, n) for n in range(5))
        beta = fresh / state[0, :, 0:1] - state[2, :, 0:1]
        guess = jnp.where(k == 0, 1.0 + (fresh - 2.0 * with_v) / of_v, 0.0)
        curve = (sums[:, 2:3] + near) + 2.0 * beta * cross + beta * beta * state[1, :, 0:1]
        alpha = fresh / curve
        for n, column in enumerate((fresh, curve, guess, alpha, beta)):
            state[n] = jnp.broadcast_to(column, (rhs, LANES))
        for leaf in range(leaves):
            p_coef = coefs[OF_V, leaf] + beta * coefs[OF_P, leaf]
            q_coef = image_coef[leaf] + beta * coefs[OF_Q, leaf]
            r_coef = coefs[OF_R, leaf] - alpha * q_coef
            coefs[OF_P, leaf] = p_coef
            coefs[OF_Q, leaf] = q_coef
            coefs[OF_R, leaf] = r_coef
            coefs[OF_V, leaf] = r_coef + guess * p_coef
        return carry

    lax.fori_loop(0, ITERS, iteration, 0)
    finish()

    sources = [block_of(gain), block_of(r_ref), block_of(p_ref)]

    def restore(group, carry):
        for n in range(4):
            ob = group * 4 + n
            span = pl.ds(pl.multiple_of(ob * LANES, LANES), LANES)
            got = pick(sources, inverse[pl.ds(ob, 1), :], 0, blocks)
            x_out[:, span] = got[0]
            r_out[:, span] = got[1]
            p_out[:, span] = got[2]
        return carry

    line_out[...] = to_tile(row_dot(r_ref[...], r_ref[...]))
    sends = line_copies(ITERS)
    for c in sends:
        c.start()
    lax.fori_loop(0, blocks // 8, restore, 0)
    for c in sends:
        c.wait()
    plane_out[...] = line_sum(line_out, line_in.at[ITERS])
    sends = plane_copies(ITERS)
    for c in sends:
        c.start()
    lax.fori_loop(blocks // 8, blocks // 4, restore, 0)
    for c in sends:
        c.wait()
    tile = line_sum(plane_out, plane_in.at[ITERS])
    ratio[...] = jnp.broadcast_to(from_tile(tile) / state[0, :, 0:1], ratio.shape)


def per_device(coords, solution, residual, direction, order, leaf_skel, local_skel, upper_skel):
    dims, count = coords.shape
    rhs = solution.shape[0]
    leaves, rank = leaf_skel.shape
    leaf_size = count // leaves
    blocks = count // LANES
    flat = jax.ShapeDtypeStruct((rhs, count), F32)
    slots = 4 * PER_ROUND + 5
    gain, resid, search, ratio = pl.pallas_call(
        solve,
        out_shape=(flat, flat, flat, jax.ShapeDtypeStruct((rhs, LANES), F32)),
        in_specs=[VMEM] * 7,
        out_specs=(VMEM,) * 4,
        scratch_shapes=[
            pltpu.VMEM((leaves, leaf_size, leaf_size), BF16),
            pltpu.VMEM((leaves, leaf_size, LANES), BF16),
            pltpu.VMEM((LANES, count), BF16),
            pltpu.VMEM((leaves, rank, leaf_size), BF16),
            pltpu.VMEM((leaves, rank, leaf_size), BF16),
            pltpu.VMEM((slots, rank, rank), BF16),
            pltpu.VMEM((slots, rank, rank), BF16),
            pltpu.VMEM((dims, count), F32),
            pltpu.VMEM((rhs, count), F32),
            pltpu.VMEM((3 * rhs, count), BF16),
            pltpu.VMEM((rhs, count), F32),
            pltpu.VMEM((rhs, count), F32),
            pltpu.VMEM((rhs, count), F32),
            pltpu.VMEM((rhs, count), F32),
            pltpu.VMEM((rhs, count), F32),
            pltpu.VMEM((2 * blocks, count), BF16),
            pltpu.VMEM((LANES, count), BF16),
            pltpu.VMEM((blocks, LANES), jnp.int32),
            pltpu.VMEM((leaves, dims, rank), F32),
            pltpu.VMEM((dims, rank), F32),
            pltpu.VMEM((5, rhs, LANES), F32),
            pltpu.VMEM((8, rhs, rank), F32),
            pltpu.VMEM((4, dims + 8, rank), F32),
            pltpu.VMEM((4, 3, dims + 8, rank), F32),
            pltpu.VMEM((4, rhs, rank), F32),
            pltpu.VMEM((ITERS, 4, 3, rhs, rank), F32),
            pltpu.VMEM((4, rhs, LANES), F32),
            pltpu.VMEM((ITERS, 4, 3, rhs, LANES), F32),
            pltpu.VMEM((4, 2, dims, rank), F32),
            pltpu.VMEM((6, leaves, rhs, rank), F32),
            pltpu.VMEM((8, LANES), F32),
            pltpu.VMEM((ITERS + 1, 15, 8, LANES), F32),
            pltpu.VMEM((8, LANES), F32),
            pltpu.VMEM((ITERS + 1, 15, 8, LANES), F32),
            pltpu.SemaphoreType.DMA((4, 3)),
            pltpu.SemaphoreType.DMA((ITERS + 1, 4, 3)),
            pltpu.SemaphoreType.DMA((4, 3)),
            pltpu.SemaphoreType.DMA((ITERS, 4, 3)),
            pltpu.SemaphoreType.DMA((15,)),
            pltpu.SemaphoreType.DMA((ITERS + 1, 15)),
            pltpu.SemaphoreType.DMA((15,)),
            pltpu.SemaphoreType.DMA((ITERS + 1, 15)),
        ],
        compiler_params=pltpu.CompilerParams(
            vmem_limit_bytes=56 * 1024 * 1024, collective_id=0, has_side_effects=True
        ),
    )(
        coords,
        residual,
        direction,
        order.reshape(blocks, LANES),
        leaf_skel,
        local_skel,
        upper_skel,
    )
    return pl.pallas_call(
        finish_state,
        out_shape=(flat, flat, flat),
        in_specs=[VMEM] * 5,
        out_specs=(VMEM,) * 3,
    )(solution, gain, resid, search, ratio)


def solution(mesh):
    in_specs = (
        P(None, "leaf"),
        P(None, "leaf"),
        P(None, "leaf"),
        P(None, "leaf"),
        P("leaf"),
        P("leaf", None),
        P("leaf", None),
        P(None, "leaf", None),
    )
    out_specs = (P(None, "leaf"), P(None, "leaf"), P(None, "leaf"))
    return jax.shard_map(
        per_device, mesh=mesh, in_specs=in_specs, out_specs=out_specs, check_vma=False
    )
```
